256 devices in a mesh: comp: 32 (over y, z), harm: 8 (over x, core).
Axes of the slice: x: 4, y: 4, z: 8, core: 2. Of those that a mesh axis runs over, the one named last changes fastest.
Arguments:
- load: float32 [128, 131072], P('harm', 'comp'), may hold values from -6 to 6
- stiff_blocks: bfloat16 [1024, 8, 128, 128], P('comp'), as said below
- mass_blocks: bfloat16 [1024, 8, 128, 128], P('comp'), as said below
- block_cols: int32 [1024, 8], P('comp'), may hold values from -8 to 1031, as said below
- contact_rows: int32 [32, 256], P('comp'), may hold values from 0 to 4095, as said below
- partner_slot: int32 [32, 256], P('comp'), may hold values from 0 to 255, each once within a row
- contact_count: int32 [32], P('comp'), may hold values from 32 to 256, as said below
- normal_load: float32 [32, 256], P('comp'), may hold values from 0.3 to 3
- contact_stiffness: float32 [32, 256], P('comp'), may hold values from 0.3 to 3
- frequency: float32 [1], replicated, may hold values from 0.2 to 1
Outputs:
- displacement: float32 [128, 131072], P('harm', 'comp')
- residual: float32 [128, 131072], P('harm', 'comp')
The draws below stay inside these ranges and needn't reach their ends.
Inputs may be any that keep to these rules, and one draw needn't show every extreme that they name: `block_cols`: entry 0 of block row r is r; its other 7 entries are distinct, differ from r by 1 to 8, and include r - 8 and r + 8; columns outside 0 .. 1023 refer to zero parts of the field. `contact_rows`: the 256 entries of one group are distinct. Slots 0 .. contact_count[d]-1 of group d are live; the others carry no force. `stiff_blocks`: slot 0 of every block row is the block on the diagonal. `mass_blocks`: slot 0 of every block row is the block on the diagonal.
All inputs are finite; a program needn't handle non-finite values.
Results may differ from the reference program's by a relative error of at most 0.015.
The reference program's roundings to bfloat16 on the way (of `rounded`) count: a program that leaves them out, or rounds other values in their place, can miss the bound.
Values may be sent and summed in bfloat16 or wider, within the bound.
No kernel may reach another device: no remote copies, remote signals or barrier semaphores. Data moves between devices by JAX's collectives and lax.ppermute only.
A program may use at most 64 MiB of HBM per device.

```python
import math
import jax
import jax.numpy as jnp
from jax import lax

H = 128
TIME_POINTS = 1024
BLK = 128
SLOTS = 8
BAND = 8
ITERS = 3
CMAX = 256
GROUPS = 32
NB = 1024
DOF_DEV = 4096
NDOF = 131072


def block_draw(key, lowest, highest, spread):
    key_one, key_two = jax.random.split(key)
    values = jnp.clip(jax.random.normal(key_one, (NB, SLOTS, BLK, BLK), jnp.float32), -6.0, 6.0)
    values = values * (spread / math.sqrt(SLOTS * BLK))
    diagonal = jax.random.uniform(key_two, (NB, BLK), jnp.float32, lowest, highest)
    values = values.at[:, 0].add(diagonal[:, :, None] * jnp.eye(BLK, dtype=jnp.float32)[None, :, :])
    return values.astype(jnp.bfloat16)


def draw_stiff_blocks(key, part):
    return block_draw(jax.random.fold_in(key, 11), 3.0, 5.0, 1.0)


def draw_mass_blocks(key, part):
    return block_draw(jax.random.fold_in(key, 23), 0.5, 1.0, 0.25)


def draw_block_cols(key, part):
    row_ids = jnp.arange(NB, dtype=jnp.int32)
    offset_pool = jnp.concatenate([jnp.arange(1 - BAND, 0, dtype=jnp.int32), jnp.arange(1, BAND, dtype=jnp.int32)])

    def one_row(row_key):
        pick_key, order_key = jax.random.split(row_key)
        picked = jax.random.permutation(pick_key, offset_pool)[:SLOTS - 3]
        others = jnp.concatenate([jnp.array([-BAND, BAND], jnp.int32), picked])
        return jnp.concatenate([jnp.zeros((1,), jnp.int32), jax.random.permutation(order_key, others)])
    offsets = jax.vmap(one_row)(jax.random.split(jax.random.fold_in(key, 31), NB))
    return row_ids[:, None] + offsets


def draw_contact_rows(key, part):
    key_one, key_two = jax.random.split(jax.random.fold_in(key, 41))
    inner_rows = jnp.arange(1, DOF_DEV - 1, dtype=jnp.int32)

    def one_device(device_key):
        pick_key, order_key, drawn_key = jax.random.split(device_key, 3)
        drawn_rows = jax.random.permutation(drawn_key, jnp.arange(DOF_DEV, dtype=jnp.int32))[:CMAX]
        chosen = jax.random.permutation(pick_key, inner_rows)[:CMAX - 2]
        with_ends = jnp.concatenate([jnp.array([0, DOF_DEV - 1], jnp.int32), chosen])
        return (drawn_rows, jax.random.permutation(order_key, with_ends))
    drawn_rows, ended = jax.vmap(one_device)(jax.random.split(key_one, GROUPS))
    marked = jax.random.randint(key_two, (), 0, GROUPS)
    return jnp.where((jnp.arange(GROUPS, dtype=jnp.int32) == marked)[:, None], ended, drawn_rows)


def draw_contact_count(key, part):
    key_one, key_two, key_three, key_four = jax.random.split(jax.random.fold_in(key, 53), 4)
    counts = jax.random.randint(key_one, (GROUPS,), CMAX // 8, CMAX // 2 + 1)
    heavy = jax.random.randint(key_two, (GROUPS,), 0, 8) == 0
    counts = jnp.where(heavy, CMAX, counts)
    busiest = jax.random.randint(key_three, (), 0, GROUPS)
    lightest = (busiest + 1 + jax.random.randint(key_four, (), 0, GROUPS - 1)) % GROUPS
    counts = counts.at[busiest].set(CMAX).at[lightest].set(CMAX // 8)
    return counts.astype(jnp.int32)


def block_levels(key, dims, pieces, low, largest):
    loudness, own = 1.0, jax.random.fold_in(key, 6)
    for axis_at, parts in pieces:
        draws = jnp.exp(jax.random.uniform(jax.random.fold_in(own, axis_at), (parts,), jnp.float32, low / len(pieces), largest / len(pieces)))
        loudness = loudness * jnp.repeat(draws, dims[axis_at] // parts).reshape([-1 if axis == axis_at else 1 for axis in range(len(dims))])
    return loudness


def centred(key, extent, width, most, cuts=(), held_as=jnp.bfloat16):
    entries = width * jax.random.normal(key, extent, jnp.float32)
    if cuts:
        entries = entries * block_levels(key, extent, cuts, -0.22, 0.18)
    return jnp.clip(entries, -most, most).astype(held_as)


def setup_inputs(seed: int = 0) -> dict:
    splits = jax.random.split(jax.random.key(seed), 11)
    load = centred(splits[0], (H, NDOF), 1.0, 6.0, ((0, 8), (1, 32)), jnp.float32)
    stiff_blocks = draw_stiff_blocks(jax.random.fold_in(splits[10], 71), 0)
    mass_blocks = draw_mass_blocks(jax.random.fold_in(splits[10], 71), 0)
    block_cols = draw_block_cols(jax.random.fold_in(splits[10], 71), 0)
    contact_rows = draw_contact_rows(jax.random.fold_in(splits[10], 71), 0)
    partner_slot = jax.vmap(lambda own: jax.random.permutation(own, CMAX))(jax.random.split(splits[5], GROUPS)).reshape((GROUPS, CMAX)).astype(jnp.int32)
    contact_count = draw_contact_count(jax.random.fold_in(splits[10], 71), 0)
    normal_load = jnp.clip(jnp.exp(math.log(3.0) - 2.3025851 * jax.random.uniform(splits[7], (GROUPS, CMAX), jnp.float32) ** block_levels(splits[7], (GROUPS, CMAX), ((0, 32),), -0.2, 0.2)), 0.3, 3.0)
    contact_stiffness = jnp.clip(jnp.exp(math.log(3.0) - 2.3025851 * jax.random.uniform(splits[8], (GROUPS, CMAX), jnp.float32) ** block_levels(splits[8], (GROUPS, CMAX), ((0, 32),), -0.2, 0.2)), 0.3, 3.0)
    frequency = jnp.clip(jax.random.uniform(splits[9], (1,), jnp.float32, 0.2, 1.0), 0.2, 1.0)
    return dict(load=load, stiff_blocks=stiff_blocks, mass_blocks=mass_blocks, block_cols=block_cols, contact_rows=contact_rows, partner_slot=partner_slot, contact_count=contact_count, normal_load=normal_load, contact_stiffness=contact_stiffness, frequency=frequency)


def harmonic_tables():
    column_list = jnp.arange(H, dtype=jnp.int32)
    harmonic_orders = jnp.where(column_list <= H // 2, column_list, column_list - H // 2).astype(jnp.int32)
    time_points = jnp.arange(TIME_POINTS, dtype=jnp.int32)
    phase_values = (time_points[:, None] * harmonic_orders[None, :]) % TIME_POINTS
    phase_angles = phase_values.astype(jnp.float32) * jnp.float32(2.0 * math.pi / TIME_POINTS)
    instant_table = jnp.where(column_list[None, :] <= H // 2, jnp.cos(phase_angles), jnp.sin(phase_angles))
    weight_factors = jnp.where(column_list == 0, jnp.float32(1.0), jnp.float32(2.0)).astype(jnp.float32) / jnp.float32(TIME_POINTS)
    return instant_table, weight_factors, harmonic_orders


def block_products(stiff_blocks, mass_blocks, block_cols, rounded):
    padded = jnp.pad(rounded.reshape(H, NB, BLK), ((0, 0), (BAND, BAND), (0, 0))).astype(jnp.float32)

    def one_row(row_index):
        stiff_row = stiff_blocks[row_index].astype(jnp.float32)
        mass_row = mass_blocks[row_index].astype(jnp.float32)
        column_row = (block_cols[row_index] + BAND).astype(jnp.int32)
        picked = jnp.take(padded, column_row, axis=1)
        stiff_out = jnp.einsum("sij,hsj->hi", stiff_row, picked, precision=lax.Precision.HIGHEST)
        mass_out = jnp.einsum("sij,hsj->hi", mass_row, picked, precision=lax.Precision.HIGHEST)
        return stiff_out, mass_out

    stiff_all, mass_all = lax.map(one_row, jnp.arange(NB, dtype=jnp.int32))
    stiff_part = jnp.transpose(stiff_all, (1, 0, 2)).reshape(H, NB * BLK)
    mass_part = jnp.transpose(mass_all, (1, 0, 2)).reshape(H, NB * BLK)
    return stiff_part, mass_part


def contact_force(displacement, contact_rows, partner_slot, contact_count, normal_load, contact_stiffness, instant_table, weight_factors):
    shaped = displacement.reshape(H, GROUPS, DOF_DEV)
    listed = jnp.take_along_axis(shaped, contact_rows[None, :, :].astype(jnp.int32), axis=2)
    partner_ids = jnp.bitwise_xor(jnp.arange(GROUPS, dtype=jnp.int32), jnp.int32(GROUPS // 2))
    facing = jnp.take_along_axis(jnp.take(listed, partner_ids, axis=1), partner_slot[None, :, :].astype(jnp.int32), axis=2)
    relative = (listed - facing).reshape(H, GROUPS * CMAX)
    time_values = jnp.dot(instant_table, relative, precision=lax.Precision.HIGHEST)
    load_part = normal_load.reshape(1, GROUPS * CMAX)
    stiff_part = contact_stiffness.reshape(1, GROUPS * CMAX)
    live_mask = (jnp.arange(CMAX, dtype=jnp.int32)[None, :] < contact_count[:, None]).reshape(1, GROUPS * CMAX)
    forces = jnp.where(live_mask, load_part * jnp.tanh(stiff_part * time_values / load_part), jnp.zeros_like(time_values))
    projected = lax.dot_general(instant_table, forces, (((0,), (0,)), ((), ())), precision=lax.Precision.HIGHEST) * weight_factors[:, None]
    targets = (jnp.arange(GROUPS, dtype=jnp.int32)[:, None] * DOF_DEV + contact_rows.astype(jnp.int32)).reshape(GROUPS * CMAX)
    return jnp.zeros((H, NDOF), projected.dtype).at[:, targets].add(projected)


def reference(load, stiff_blocks, mass_blocks, block_cols, contact_rows, partner_slot, contact_count, normal_load, contact_stiffness, frequency):
    instant_table, weight_factors, harmonic_orders = harmonic_tables()
    factor = frequency[0] * harmonic_orders.astype(jnp.float32) * jnp.float32(2.0 / H)
    factor = factor * factor
    stiff_diag = jnp.diagonal(stiff_blocks[:, 0], axis1=1, axis2=2).astype(jnp.float32).reshape(NDOF)
    mass_diag = jnp.diagonal(mass_blocks[:, 0], axis1=1, axis2=2).astype(jnp.float32).reshape(NDOF)
    dynamic = stiff_diag[None, :] - factor[:, None] * mass_diag[None, :]
    displacement = load / dynamic
    residual = jnp.zeros_like(displacement)
    for sweep_index in range(ITERS):
        rounded = displacement.astype(jnp.bfloat16)
        gap = displacement - lax.optimization_barrier(rounded).astype(jnp.float32)
        stiff_part, mass_part = block_products(stiff_blocks, mass_blocks, block_cols, rounded)
        stiff_part = stiff_part + stiff_diag[None, :] * gap
        mass_part = mass_part + mass_diag[None, :] * gap
        applied = stiff_part - factor[:, None] * mass_part
        nonlinear = contact_force(displacement, contact_rows, partner_slot, contact_count, normal_load, contact_stiffness, instant_table, weight_factors)
        residual = load - applied - nonlinear
        displacement = displacement + residual / dynamic
    return displacement, residual
```

```python
import functools
import math

import jax
import jax.numpy as jnp
import ml_dtypes
import numpy as np
from jax import lax
from jax.experimental import pallas as pl
from jax.experimental.pallas import tpu as pltpu
from jax.sharding import PartitionSpec as P

H = 128
TIME_POINTS = 1024
BLK = 128
SLOTS = 8
BAND = 8
ITERS = 3
OWN = 16
ROWS = 32
CMAX = 256
DOFS = ROWS * BLK
F32 = jnp.float32
BF16 = jnp.bfloat16
LAST_LAST = (((1,), (1,)), ((), ()))

VM = pl.BlockSpec(memory_space=pltpu.VMEM)
SM = pl.BlockSpec(memory_space=pltpu.SMEM)
ANY = pl.BlockSpec(memory_space=pl.ANY)


def tables():
    j = np.arange(H)
    waves = np.where(j <= H // 2, j, j - H // 2)
    phase = (np.arange(TIME_POINTS)[:, None] * waves[None, :]) % TIME_POINTS
    angle = phase.astype(np.float64) * (2.0 * math.pi / TIME_POINTS)
    table = np.where(j[None, :] <= H // 2, np.cos(angle), np.sin(angle)).astype(np.float32)
    high = table.astype(ml_dtypes.bfloat16)
    low = (table - high.astype(np.float32)).astype(ml_dtypes.bfloat16)
    forward = np.concatenate([high, high, low], axis=1)
    weights = (np.where(j == 0, 1.0, 2.0) / TIME_POINTS).astype(np.float32)
    back = (table * weights[None, :]).T
    back_high = back.astype(ml_dtypes.bfloat16)
    back_low = (back - back_high.astype(np.float32)).astype(ml_dtypes.bfloat16)
    backward = np.concatenate(
        [
            back_high.reshape(H // OWN, OWN, TIME_POINTS),
            back_low.reshape(H // OWN, OWN, TIME_POINTS),
        ],
        axis=1,
    )
    return forward, backward


def dot(a, b):
    return jnp.dot(a, b, preferred_element_type=F32)


def dot_nt(a, b):
    return lax.dot_general(a, b, LAST_LAST, preferred_element_type=F32)


def split3(x):
    high = x.astype(BF16)
    rest = x - high.astype(F32)
    mid = rest.astype(BF16)
    low = (rest - mid.astype(F32)).astype(BF16)
    return jnp.concatenate([high, mid, low], axis=0)


def sum3(y):
    n = y.shape[0] // 3
    return y[:n] + y[n : 2 * n] + y[2 * n :]


def own_factor(freq, place):
    j = place[0] * OWN + lax.broadcasted_iota(jnp.int32, (OWN, BLK), 0)
    waves = jnp.where(j <= H // 2, j, j - H // 2)
    factor = freq[0] * waves.astype(F32) * (2.0 / H)
    return factor * factor


def cols_of(r):
    return pl.ds(pl.multiple_of(r * BLK, BLK), BLK)


def init_kernel(
    freq, place, load, stiff, mass, rows, pslot, normal, tangent, count,
    disp_o, inner_o, first_o, last_o, dyn_o, inv_o, hot_o, swap_o, listed_o, inv_rows_o, ratio_o, limit_o,
    s_buf, m_buf, sems,
):
    copy_s = pltpu.make_async_copy(stiff.at[:, 0], s_buf, sems.at[0])
    copy_m = pltpu.make_async_copy(mass.at[:, 0], m_buf, sems.at[1])
    copy_s.start()
    copy_m.start()
    factor = own_factor(freq, place)
    in_block = lax.broadcasted_iota(jnp.int32, (BLK, CMAX), 0)
    wanted = rows[...]
    for r in range(ROWS):
        hot_o[r] = jnp.where(in_block + r * BLK == wanted, 1.0, 0.0).astype(BF16)
    swap_o[...] = jnp.where(
        lax.broadcasted_iota(jnp.int32, (CMAX, CMAX), 0) == pslot[...], 1.0, 0.0
    ).astype(BF16)
    ratio_o[...] = tangent[...] / normal[...]
    live = lax.broadcasted_iota(jnp.int32, (1, CMAX), 1) < count[0]
    limit_o[...] = jnp.where(live, normal[...], 0.0)
    eye = lax.broadcasted_iota(jnp.int32, (BLK, BLK), 0) == lax.broadcasted_iota(
        jnp.int32, (BLK, BLK), 1
    )
    ones = jnp.ones((OWN, BLK), BF16)
    zero = jnp.zeros((BLK, BLK), BF16)
    copy_s.wait()
    copy_m.wait()
    listed = jnp.zeros((3 * OWN, CMAX), F32)
    dyn_rows = jnp.zeros((3 * OWN, CMAX), F32)
    for r in range(ROWS):
        s_diag = dot(ones, jnp.where(eye, s_buf[r], zero))
        m_diag = dot(ones, jnp.where(eye, m_buf[r], zero))
        dynamic = s_diag - factor * m_diag
        at = slice(r * BLK, (r + 1) * BLK)
        disp = load[:, at] / dynamic
        rounded = disp.astype(BF16)
        dyn_o[:, at] = dynamic
        inv_o[:, at] = 1.0 / dynamic
        disp_o[:, at] = disp
        inner_o[r] = rounded
        if r < BAND:
            first_o[r] = rounded
        if r >= ROWS - BAND:
            last_o[r - (ROWS - BAND)] = rounded
        listed = listed + dot(split3(disp), hot_o[r])
        dyn_rows = dyn_rows + dot(split3(dynamic), hot_o[r])
    listed_o[...] = sum3(listed)
    inv_rows_o[...] = 1.0 / sum3(dyn_rows)


def relative_kernel(place, own, core, own_far, core_far, swap, ratio, out):
    far = jnp.concatenate([split3(own_far[...]), split3(core_far[...])], axis=0)
    facing = dot(far, swap[...])
    scale = ratio[...]
    side = lax.rem(place[0], 2)
    out[pl.ds(pl.multiple_of(side * OWN, OWN), OWN), :] = (own[...] - sum3(facing[: 3 * OWN])) * scale
    out[pl.ds(pl.multiple_of((1 - side) * OWN, OWN), OWN), :] = (
        core[...] - sum3(facing[3 * OWN :])
    ) * scale


def product_kernel(
    cols, freq, place, inner, before, after, stiff, mass, load, disp, dyn, inv, hot, lin_o, listed_o, field, *, final
):
    field[:BAND] = before[...]
    field[BAND : BAND + ROWS] = inner[...]
    field[BAND + ROWS :] = after[...]
    factor = own_factor(freq, place)

    def row(r, listed):
        picked = jnp.concatenate([field[cols[r, s]] for s in range(SLOTS)], axis=1)
        both = jnp.concatenate(
            [jnp.concatenate([stiff[r, s], mass[r, s]], axis=0) for s in range(SLOTS)], axis=1
        )
        made = dot_nt(picked, both)
        applied = made[:, :BLK] - factor * made[:, BLK:]
        at = cols_of(r)
        rounded = inner[r].astype(F32)
        if final:
            lin_o[:, at] = load[:, at] - (applied + dyn[:, at] * (disp[:, at] - rounded))
            return listed
        lin = rounded + (load[:, at] - applied) * inv[:, at]
        lin_o[:, at] = lin
        return listed + dot(split3(lin), hot[r])

    listed = lax.fori_loop(0, ROWS, row, jnp.zeros((3 * OWN, CMAX), F32), unroll=8)
    listed_o[...] = sum3(listed)


def time_kernel(place, own, one, two, three, forward, backward, limit, lin_rows, inv_rows, force_o, listed_o, rel):
    chunk = place[0] // 2
    for piece, away in ((own, 0), (one, 3), (two, 2), (three, 1)):
        at = lax.rem(chunk + away, 4) * 32
        rel[pl.ds(pl.multiple_of(at, 32), 32), :] = piece[...]
    whole = rel[...]
    high = whole.astype(BF16)
    low = (whole - high.astype(F32)).astype(BF16)
    stacked = jnp.concatenate([high, low, high], axis=0)
    step = 256
    total = jnp.zeros((2 * OWN, CMAX), F32)
    for n in range(0, TIME_POINTS, step):
        values = jnp.tanh(dot(forward[n : n + step, :], stacked)).astype(BF16)
        total = total + dot(backward[:, n : n + step], values)
    force = (total[:OWN] + total[OWN:]) * limit[...]
    force_o[...] = force
    listed_o[...] = lin_rows[...] - force * inv_rows[...]


def spread(force, hot_block):
    high = force.astype(BF16)
    low = (force - high.astype(F32)).astype(BF16)
    both = dot_nt(jnp.concatenate([high, low], axis=0), hot_block)
    return both[:OWN] + both[OWN:]


def update_kernel(force, hot, lin, inv, disp_o, inner_o, first_o, last_o):
    add = force[...]
    for r in range(ROWS):
        at = slice(r * BLK, (r + 1) * BLK)
        disp = lin[:, at] - spread(add, hot[r]) * inv[:, at]
        rounded = disp.astype(BF16)
        disp_o[:, at] = disp
        inner_o[r] = rounded
        if r < BAND:
            first_o[r] = rounded
        if r >= ROWS - BAND:
            last_o[r - (ROWS - BAND)] = rounded


def finish_kernel(force, hot, lin, inv, disp, disp_o, residual_o):
    add = force[...]
    for r in range(ROWS):
        at = slice(r * BLK, (r + 1) * BLK)
        residual = lin[:, at] - spread(add, hot[r])
        residual_o[:, at] = residual
        disp_o[:, at] = disp[:, at] + residual * inv[:, at]


def shape(dims, dtype=F32):
    return jax.ShapeDtypeStruct(dims, dtype)


def params():
    return pltpu.CompilerParams(vmem_limit_bytes=48 << 20)


FULL = (OWN, DOFS)
LIST = (OWN, CMAX)
EDGE = (BAND, OWN, BLK)


def local(
    load,
    stiff_blocks,
    mass_blocks,
    block_cols,
    contact_rows,
    partner_slot,
    contact_count,
    normal_load,
    contact_stiffness,
    frequency,
):
    harm = lax.axis_index("harm").astype(jnp.int32)
    place = harm.reshape(1)
    groups = lax.axis_size("comp")
    devices = lax.axis_size("harm")
    local_cols = block_cols - lax.axis_index("comp") * ROWS + BAND
    forward, backward = tables()
    forward = jnp.asarray(forward)
    backward = lax.dynamic_index_in_dim(jnp.asarray(backward), harm, 0, keepdims=False)

    (
        disp, inner, first, last, dyn, inv, hot, swap, listed, inv_rows, ratio, limit
    ) = pl.pallas_call(
        init_kernel,
        out_shape=(
            shape(FULL), shape((ROWS, OWN, BLK), BF16), shape(EDGE, BF16), shape(EDGE, BF16),
            shape(FULL), shape(FULL), shape((ROWS, BLK, CMAX), BF16), shape((CMAX, CMAX), BF16),
            shape(LIST), shape(LIST), shape((1, CMAX)), shape((1, CMAX)),
        ),
        in_specs=[SM, SM, VM, ANY, ANY, VM, VM, VM, VM, SM],
        out_specs=(VM,) * 12,
        scratch_shapes=[
            pltpu.VMEM((ROWS, BLK, BLK), BF16),
            pltpu.VMEM((ROWS, BLK, BLK), BF16),
            pltpu.SemaphoreType.DMA((2,)),
        ],
        compiler_params=params(),
        name="init",
    )(frequency, place, load, stiff_blocks, mass_blocks, contact_rows, partner_slot, normal_load, contact_stiffness, contact_count)

    across = groups // 2
    far = [(i, i ^ across) for i in range(groups)]
    far_core = [
        (g * devices + d, (g ^ across) * devices + (d ^ 1))
        for g in range(groups)
        for d in range(devices)
    ]
    core = [(i, i ^ 1) for i in range(devices)]
    up = [(i, i + 1) for i in range(groups - 1)]
    down = [(i + 1, i) for i in range(groups - 1)]

    def around(x, steps):
        return lax.ppermute(x, "harm", [(i, (i + steps) % devices) for i in range(devices)])

    for sweep in range(ITERS):
        final = sweep == ITERS - 1
        own_far = lax.ppermute(listed, "comp", far)
        core_far = lax.ppermute(listed, ("comp", "harm"), far_core)
        core_own = lax.ppermute(listed, "harm", core)
        before = lax.ppermute(last, "comp", up)
        after = lax.ppermute(first, "comp", down)
        relative = pl.pallas_call(
            relative_kernel,
            out_shape=shape((2 * OWN, CMAX)),
            in_specs=[SM] + [VM] * 6,
            out_specs=VM,
            compiler_params=params(),
            name="relative",
        )(place, listed, core_own, own_far, core_far, swap, ratio)
        one = around(relative, 2)
        two = around(relative, 4)
        three = around(relative, 6)
        lin, lin_rows = pl.pallas_call(
            functools.partial(product_kernel, final=final),
            out_shape=(shape(FULL), shape(LIST)),
            in_specs=[SM, SM, SM] + [VM] * 10,
            out_specs=(VM, VM),
            scratch_shapes=[pltpu.VMEM((ROWS + 2 * BAND, OWN, BLK), BF16)],
            compiler_params=params(),
            cost_estimate=pl.CostEstimate(flops=270_000_000, bytes_accessed=17_000_000, transcendentals=0),
            name="product",
        )(local_cols, frequency, place, inner, before, after, stiff_blocks, mass_blocks, load, disp, dyn, inv, hot)
        force, listed = pl.pallas_call(
            time_kernel,
            out_shape=(shape(LIST), shape(LIST)),
            in_specs=[SM] + [VM] * 9,
            out_specs=(VM, VM),
            scratch_shapes=[pltpu.VMEM((H, CMAX), F32)],
            compiler_params=params(),
            name="time",
        )(place, relative, one, two, three, forward, backward, limit, lin_rows, inv_rows)
        if final:
            return pl.pallas_call(
                finish_kernel,
                out_shape=(shape(FULL), shape(FULL)),
                in_specs=[VM] * 5,
                out_specs=(VM, VM),
                compiler_params=params(),
                name="finish",
            )(force, hot, lin, inv, disp)
        disp, inner, first, last = pl.pallas_call(
            update_kernel,
            out_shape=(shape(FULL), shape((ROWS, OWN, BLK), BF16), shape(EDGE, BF16), shape(EDGE, BF16)),
            in_specs=[VM] * 4,
            out_specs=(VM,) * 4,
            compiler_params=params(),
            name="update",
        )(force, hot, lin, inv)


def solution(mesh):
    placed = (
        P("harm", "comp"),
        P("comp", None, None, None),
        P("comp", None, None, None),
        P("comp", None),
        P("comp", None),
        P("comp", None),
        P("comp"),
        P("comp", None),
        P("comp", None),
        P(),
    )
    return jax.shard_map(
        local,
        mesh=mesh,
        in_specs=placed,
        out_specs=(P("harm", "comp"), P("harm", "comp")),
        check_vma=False,
    )
```

```python
import functools
import math

import jax
import jax.numpy as jnp
import ml_dtypes
import numpy as np
from jax import lax
from jax.experimental import pallas as pl
from jax.experimental.pallas import tpu as pltpu
from jax.sharding import PartitionSpec as P

H = 128
TIME_POINTS = 1024
BLK = 128
SLOTS = 8
BAND = 8
ITERS = 3
OWN = 16
ROWS = 32
HALF = ROWS // 2
RATIO = 16
LIMIT = 24
CMAX = 256
DOFS = ROWS * BLK
F32 = jnp.float32
BF16 = jnp.bfloat16
LAST_LAST = (((1,), (1,)), ((), ()))

VM = pl.BlockSpec(memory_space=pltpu.VMEM)
SM = pl.BlockSpec(memory_space=pltpu.SMEM)
FAR = pl.BlockSpec(memory_space=pltpu.HBM)


def tables():
    j = np.arange(H)
    waves = np.where(j <= H // 2, j, j - H // 2)
    phase = (np.arange(TIME_POINTS)[:, None] * waves[None, :]) % TIME_POINTS
    angle = phase.astype(np.float64) * (2.0 * math.pi / TIME_POINTS)
    table = np.where(j[None, :] <= H // 2, np.cos(angle), np.sin(angle)).astype(np.float32)
    high = table.astype(ml_dtypes.bfloat16)
    low = (table - high.astype(np.float32)).astype(ml_dtypes.bfloat16)
    forward = np.concatenate([high, high, low], axis=1)
    weights = (np.where(j == 0, 1.0, 2.0) / TIME_POINTS).astype(np.float32)
    back = (table * weights[None, :]).T
    back_high = back.astype(ml_dtypes.bfloat16)
    back_low = (back - back_high.astype(np.float32)).astype(ml_dtypes.bfloat16)
    backward = np.concatenate(
        [
            back_high.reshape(H // OWN, OWN, TIME_POINTS),
            back_low.reshape(H // OWN, OWN, TIME_POINTS),
        ],
        axis=1,
    )
    return forward, backward


def dot(a, b):
    return jnp.dot(a, b, preferred_element_type=F32)


def dot_nt(a, b):
    return lax.dot_general(a, b, LAST_LAST, preferred_element_type=F32)


def split3(x):
    high = x.astype(BF16)
    rest = x - high.astype(F32)
    mid = rest.astype(BF16)
    low = (rest - mid.astype(F32)).astype(BF16)
    return jnp.concatenate([high, mid, low], axis=0)


def sum3(y):
    n = y.shape[0] // 3
    return y[:n] + y[n : 2 * n] + y[2 * n :]


def own_factor(freq, place):
    j = place[0] * OWN + lax.broadcasted_iota(jnp.int32, (OWN, BLK), 0)
    waves = jnp.where(j <= H // 2, j, j - H // 2)
    factor = freq[0] * waves.astype(F32) * (2.0 / H)
    return factor * factor


def cols_of(r):
    return pl.ds(pl.multiple_of(r * BLK, BLK), BLK)


def put_edges(place, inner, even_o, odd_o):
    low, high = slice(0, BAND), slice(ROWS - BAND, ROWS)
    side = lax.rem(place[1], 2)

    @pl.when(side == 0)
    def _():
        even_o[...] = inner[high]
        odd_o[...] = inner[low]

    @pl.when(side == 1)
    def _():
        even_o[...] = inner[low]
        odd_o[...] = inner[high]


def init_kernel(
    freq, place, count, load, stiff, mass, rows, pslot, normal, tangent,
    disp_o, inner_o, even_o, odd_o, dyn_o, inv_o, hot_o, swap_o, listed_o, aux_o,
    s_buf, m_buf, l_buf, small_i, small_f, parts, sems,
):
    moves = [
        pltpu.make_async_copy(rows, small_i.at[0], sems.at[0]),
        pltpu.make_async_copy(pslot, small_i.at[1], sems.at[1]),
        pltpu.make_async_copy(normal, small_f.at[0], sems.at[2]),
        pltpu.make_async_copy(tangent, small_f.at[1], sems.at[3]),
        pltpu.make_async_copy(stiff.at[:, 0], s_buf, sems.at[4]),
        pltpu.make_async_copy(mass.at[:, 0], m_buf, sems.at[5]),
        pltpu.make_async_copy(load, l_buf, sems.at[6]),
    ]
    for move in moves:
        move.start()
    factor = own_factor(freq, place)
    for move in moves[:4]:
        move.wait()
    in_block = lax.broadcasted_iota(jnp.int32, (BLK, CMAX), 0)
    wanted = small_i[0]
    for r in range(ROWS):
        hot_o[r * BLK : (r + 1) * BLK, :] = jnp.where(in_block + r * BLK == wanted, 1.0, 0.0).astype(BF16)
    swap_o[...] = jnp.where(
        lax.broadcasted_iota(jnp.int32, (CMAX, CMAX), 0) == small_i[1], 1.0, 0.0
    ).astype(BF16)
    live = lax.broadcasted_iota(jnp.int32, (1, CMAX), 1) < count[0]
    aux_o[RATIO : RATIO + 1, :] = small_f[1] / small_f[0]
    aux_o[LIMIT : LIMIT + 1, :] = jnp.where(live, small_f[0], 0.0)
    eye = lax.broadcasted_iota(jnp.int32, (BLK, BLK), 0) == lax.broadcasted_iota(
        jnp.int32, (BLK, BLK), 1
    )
    ones = jnp.ones((OWN, BLK), BF16)
    zero = jnp.zeros((BLK, BLK), BF16)
    for move in moves[4:]:
        move.wait()
    for r in range(ROWS):
        s_diag = dot(ones, jnp.where(eye, s_buf[r], zero))
        m_diag = dot(ones, jnp.where(eye, m_buf[r], zero))
        dynamic = s_diag - factor * m_diag
        at = slice(r * BLK, (r + 1) * BLK)
        disp = l_buf[:, at] / dynamic
        dyn_o[:, at] = dynamic
        inv_o[:, at] = 1.0 / dynamic
        disp_o[:, at] = disp
        inner_o[r] = disp.astype(BF16)
        parts[: 3 * OWN, at] = split3(disp)
        parts[3 * OWN :, at] = split3(dynamic)
    listed = dot(parts[...], hot_o[...])
    listed_o[...] = sum3(listed[: 3 * OWN])
    aux_o[:OWN, :] = 1.0 / sum3(listed[3 * OWN :])
    put_edges(place, inner_o, even_o, odd_o)


def relative_kernel(own, far, swap, aux, _, out):
    facing = dot(split3(far[...]), swap[...])
    out[...] = (own[...] - sum3(facing)) * aux[RATIO : RATIO + 1, :]


def fill_field(place, inner, even, odd, field):
    side = lax.rem(place[1], 2)
    field[BAND : BAND + ROWS] = inner[...]
    far_end = BAND + ROWS
    field[pl.ds((1 - side) * far_end, BAND)] = even[...]
    field[pl.ds(side * far_end, BAND)] = odd[...]


def product_kernel(*refs, start, first, final, more):
    refs = list(refs)
    cols, freq, place, inner, even, odd = refs[:6]
    del refs[:6]
    if first:
        stiff, mass = refs[:2]
        del refs[:2]
    else:
        wide = refs.pop(0)
    load, hot, scale = refs[:3]
    del refs[:3]
    if final:
        disp = refs.pop(0)
    if more:
        earlier = refs.pop(0)
    lin_o = refs.pop(0)
    if not final:
        listed_o = refs.pop(0)
    if first:
        wide = refs.pop(0)
    field, parts = refs
    fill_field(place, inner, even, odd, field)
    factor = own_factor(freq, place)
    offset = place[1] * ROWS - BAND

    def row(i, carry):
        r = i + start
        at = cols_of(r)
        here = cols_of(i)
        picked = [field[cols[s, r] - offset] for s in range(SLOTS)]
        if first:
            for s in range(SLOTS):
                wide[i, s * BLK : (s + 1) * BLK, :BLK] = stiff[r, s].T
                wide[i, s * BLK : (s + 1) * BLK, BLK:] = mass[r, s].T
        made = dot(jnp.concatenate(picked, axis=1), wide[i])
        applied = made[:, :BLK] - factor * made[:, BLK:]
        rounded = inner[r].astype(F32)
        if final:
            lin_o[:, here] = load[:, at] - (applied + scale[:, at] * (disp[:, at] - rounded))
            return carry
        lin = rounded + (load[:, at] - applied) * scale[:, at]
        lin_o[:, here] = lin
        parts[:, here] = split3(lin)
        return carry

    lax.fori_loop(0, HALF, row, 0, unroll=HALF // 2 if first else HALF)
    if not final:
        made = sum3(dot(parts[...], hot[start * BLK : (start + HALF) * BLK, :]))
        listed_o[...] = made + earlier[...] if more else made


def time_kernel(place, near, side, across, forward, backward, aux, *rest, final):
    rel = rest[-1]
    me = place[0]
    for ref, at, other in (
        (near, 0, 0), (near, 1, 1), (side, 0, 2), (side, 1, 3),
        (across, 0, 6), (across, 1, 7), (across, 2, 4), (across, 3, 5),
    ):
        to = pl.multiple_of(jnp.bitwise_xor(me, other) * OWN, OWN)
        rel[pl.ds(to, OWN), :] = ref[at * OWN : (at + 1) * OWN, :]
    whole = rel[...]
    high = whole.astype(BF16)
    low = (whole - high.astype(F32)).astype(BF16)
    stacked = jnp.concatenate([high, low, high], axis=0)
    step = 256
    total = jnp.zeros((2 * OWN, CMAX), F32)
    for n in range(0, TIME_POINTS, step):
        values = jnp.tanh(dot(forward[n : n + step, :], stacked)).astype(BF16)
        total = total + dot(backward[me, :, n : n + step], values)
    force = (total[:OWN] + total[OWN:]) * aux[LIMIT : LIMIT + 1, :]
    if final:
        rest[0][...] = force
        return
    lin_rows, force_o, listed_o, _ = rest
    force_o[...] = force
    listed_o[...] = lin_rows[...] - force * aux[:OWN, :]


def spread(force, hot_block):
    high = force.astype(BF16)
    low = (force - high.astype(F32)).astype(BF16)
    both = dot_nt(jnp.concatenate([high, low], axis=0), hot_block)
    return both[:OWN] + both[OWN:]


def update_kernel(place, force, hot, lin_a, lin_b, inv, disp_o, inner_o, even_o, odd_o):
    add = force[...]
    for r in range(ROWS):
        at = slice(r * BLK, (r + 1) * BLK)
        here = slice(r % HALF * BLK, (r % HALF + 1) * BLK)
        lin = (lin_a if r < HALF else lin_b)[:, here]
        disp = lin - spread(add, hot[at, :]) * inv[:, at]
        disp_o[:, at] = disp
        inner_o[r] = disp.astype(BF16)
    put_edges(place, inner_o, even_o, odd_o)


def finish_kernel(force, hot, lin_a, lin_b, inv, disp, disp_o, residual_o):
    add = force[...]
    for r in range(ROWS):
        at = slice(r * BLK, (r + 1) * BLK)
        here = slice(r % HALF * BLK, (r % HALF + 1) * BLK)
        lin = (lin_a if r < HALF else lin_b)[:, here]
        residual = lin - spread(add, hot[at, :])
        residual_o[:, at] = residual
        disp_o[:, at] = disp[:, at] + residual * inv[:, at]


def shape(dims, dtype=F32):
    return jax.ShapeDtypeStruct(dims, dtype)


def held(dims, dtype=F32):
    return pltpu.VMEM(dims, dtype)


def params(limit=16):
    return pltpu.CompilerParams(vmem_limit_bytes=limit << 20)


def cost(us):
    return pl.CostEstimate(flops=int(us * 1.0e9), bytes_accessed=int(us * 3.0e6), transcendentals=0)


FULL = (OWN, DOFS)
PART = (OWN, HALF * BLK)
LIST = (OWN, CMAX)
EDGE = (BAND, OWN, BLK)
BLOCKED = (ROWS, OWN, BLK)
WIDE = (HALF, SLOTS * BLK, 2 * BLK)


def local(
    load,
    stiff_blocks,
    mass_blocks,
    block_cols,
    contact_rows,
    partner_slot,
    contact_count,
    normal_load,
    contact_stiffness,
    frequency,
):
    harm = lax.axis_index("harm").astype(jnp.int32)
    comp = lax.axis_index("comp").astype(jnp.int32)
    place = jnp.stack([harm, comp])
    groups = lax.axis_size("comp")
    devices = lax.axis_size("harm")
    cols = block_cols.T
    forward, backward = (jnp.asarray(t) for t in tables())
    stiff_near = pltpu.with_memory_space_constraint(stiff_blocks, pltpu.VMEM)
    mass_near = pltpu.with_memory_space_constraint(mass_blocks, pltpu.VMEM)

    disp, inner, even, odd, dyn, inv, hot, swap, listed, aux = pl.pallas_call(
        init_kernel,
        out_shape=(
            shape(FULL), shape(BLOCKED, BF16), shape(EDGE, BF16), shape(EDGE, BF16),
            shape(FULL), shape(FULL), shape((DOFS, CMAX), BF16), shape((CMAX, CMAX), BF16),
            shape(LIST), shape((32, CMAX)),
        ),
        in_specs=[SM, SM, SM] + [FAR] * 7,
        out_specs=(VM,) * 10,
        scratch_shapes=[
            pltpu.VMEM((ROWS, BLK, BLK), BF16),
            pltpu.VMEM((ROWS, BLK, BLK), BF16),
            pltpu.VMEM(FULL, F32),
            pltpu.VMEM((2, 1, CMAX), jnp.int32),
            pltpu.VMEM((2, 1, CMAX), F32),
            pltpu.VMEM((6 * OWN, DOFS), BF16),
            pltpu.SemaphoreType.DMA((7,)),
        ],
        compiler_params=params(),
        cost_estimate=cost(3.0),
        name="init",
    )(
        frequency, place, contact_count, *(
            pltpu.with_memory_space_constraint(x, pltpu.HBM)
            for x in (load, stiff_blocks, mass_blocks, contact_rows, partner_slot, normal_load, contact_stiffness)
        )
    )

    across = groups // 2
    far = [(i, i ^ across) for i in range(groups)]
    evens = [(i, i ^ 1) for i in range(groups)]
    odds = [(i, j) for i in range(groups) if 0 <= (j := i - 1 + 2 * (i % 2)) < groups]

    def flipped(x, bits):
        return lax.ppermute(x, "harm", [(i, i ^ bits) for i in range(devices)])

    for sweep in range(ITERS):
        first, final = sweep == 0, sweep == ITERS - 1
        own_far = lax.ppermute(listed, "comp", far)
        even_in = lax.ppermute(even, "comp", evens)
        odd_in = lax.ppermute(odd, "comp", odds)
        relative = pl.pallas_call(
            relative_kernel,
            out_shape=shape(LIST),
            in_specs=[VM] * 5,
            out_specs=VM,
            compiler_params=params(),
            cost_estimate=cost(0.2),
            name="relative",
        )(listed, own_far, swap, aux, even)
        near = jnp.concatenate([relative, flipped(relative, 1)], axis=0)
        side = flipped(near, 2)
        opposite = flipped(jnp.concatenate([near, side], axis=0), 6)
        lins, found = [], []
        for half in range(2):
            take = [cols, frequency, place, inner, even_in, odd_in]
            specs = [SM] * 3 + [VM] * 3
            if first:
                take += [stiff_near, mass_near]
                specs += [VM] * 2
            else:
                take += [wides[half]]
                specs += [VM]
            take += [load, hot, dyn if final else inv]
            specs += [VM] * 3
            if final:
                take += [disp]
                specs += [VM]
            elif half:
                take += [found[0]]
                specs += [VM]
            give = [shape(PART)] + ([] if final else [shape(LIST)])
            given = [VM] * len(give)
            if first:
                give += [held(WIDE, BF16)]
                given += [VM]
            outs = pl.pallas_call(
                functools.partial(
                    product_kernel, start=half * HALF, first=first, final=final, more=half == 1 and not final
                ),
                out_shape=tuple(give),
                in_specs=specs,
                out_specs=tuple(given),
                scratch_shapes=[
                    pltpu.VMEM((ROWS + 2 * BAND, OWN, BLK), BF16),
                    pltpu.VMEM((3 * OWN, HALF * BLK), BF16),
                ],
                compiler_params=params(),
                cost_estimate=cost(3.0 if first else 1.4),
                name="product",
            )(*take)
            lins.append(outs[0])
            if not final:
                found.append(outs[1])
            if first:
                wides = [outs[2]] if half == 0 else wides + [outs[2]]
        timed = pl.pallas_call(
            functools.partial(time_kernel, final=final),
            out_shape=(shape(LIST),) * (1 if final else 2),
            in_specs=[SM] + [VM] * (6 if final else 7),
            out_specs=(VM,) * (1 if final else 2),
            scratch_shapes=[pltpu.VMEM((H, CMAX), F32)],
            compiler_params=params(),
            cost_estimate=cost(1.0),
            name="time",
        )(place, near, side, opposite, forward, backward, aux, *([] if final else found[1:]))
        if final:
            return pl.pallas_call(
                finish_kernel,
                out_shape=(shape(FULL), shape(FULL)),
                in_specs=[VM] * 6,
                out_specs=(VM, VM),
                compiler_params=params(),
                name="finish",
            )(timed[0], hot, *lins, inv, disp)
        force, listed = timed
        disp, inner, even, odd = pl.pallas_call(
            update_kernel,
            out_shape=(shape(FULL), shape(BLOCKED, BF16), shape(EDGE, BF16), shape(EDGE, BF16)),
            in_specs=[SM] + [VM] * 5,
            out_specs=(VM,) * 4,
            compiler_params=params(),
            cost_estimate=cost(0.8),
            name="update",
        )(place, force, hot, *lins, inv)


def solution(mesh):
    placed = (
        P("harm", "comp"),
        P("comp", None, None, None),
        P("comp", None, None, None),
        P("comp", None),
        P("comp", None),
        P("comp", None),
        P("comp"),
        P("comp", None),
        P("comp", None),
        P(),
    )
    return jax.shard_map(
        local,
        mesh=mesh,
        in_specs=placed,
        out_specs=(P("harm", "comp"), P("harm", "comp")),
        check_vma=False,
    )
```

```python
import functools
import math

import jax
import jax.numpy as jnp
import ml_dtypes
import numpy as np
from jax import lax
from jax.experimental import pallas as pl
from jax.experimental.pallas import tpu as pltpu
from jax.sharding import PartitionSpec as P

H = 128
TIME_POINTS = 1024
BLK = 128
SLOTS = 8
BAND = 8
ITERS = 3
OWN = 16
ROWS = 32
HALF = ROWS // 2
RATIO = 16
LIMIT = 24
CMAX = 256
DOFS = ROWS * BLK
F32 = jnp.float32
BF16 = jnp.bfloat16
LAST_LAST = (((1,), (1,)), ((), ()))

VM = pl.BlockSpec(memory_space=pltpu.VMEM)
SM = pl.BlockSpec(memory_space=pltpu.SMEM)
FAR = pl.BlockSpec(memory_space=pltpu.HBM)


def tables():
    j = np.arange(H)
    waves = np.where(j <= H // 2, j, j - H // 2)
    phase = (np.arange(TIME_POINTS)[:, None] * waves[None, :]) % TIME_POINTS
    angle = phase.astype(np.float64) * (2.0 * math.pi / TIME_POINTS)
    table = np.where(j[None, :] <= H // 2, np.cos(angle), np.sin(angle)).astype(np.float32)
    high = table.astype(ml_dtypes.bfloat16)
    low = (table - high.astype(np.float32)).astype(ml_dtypes.bfloat16)
    forward = np.concatenate([high, high, low], axis=1)
    weights = (np.where(j == 0, 1.0, 2.0) / TIME_POINTS).astype(np.float32)
    back = (table * weights[None, :]).T
    back_high = back.astype(ml_dtypes.bfloat16)
    back_low = (back - back_high.astype(np.float32)).astype(ml_dtypes.bfloat16)
    backward = np.concatenate(
        [
            back_high.reshape(H // OWN, OWN, TIME_POINTS),
            back_low.reshape(H // OWN, OWN, TIME_POINTS),
        ],
        axis=1,
    )
    return forward, backward


def dot(a, b):
    return jnp.dot(a, b, preferred_element_type=F32)


def dot_nt(a, b):
    return lax.dot_general(a, b, LAST_LAST, preferred_element_type=F32)


def split3(x):
    high = x.astype(BF16)
    rest = x - high.astype(F32)
    mid = rest.astype(BF16)
    low = (rest - mid.astype(F32)).astype(BF16)
    return jnp.concatenate([high, mid, low], axis=0)


def sum3(y):
    n = y.shape[0] // 3
    return y[:n] + y[n : 2 * n] + y[2 * n :]


def own_factor(freq, place):
    j = place[0] * OWN + lax.broadcasted_iota(jnp.int32, (OWN, BLK), 0)
    waves = jnp.where(j <= H // 2, j, j - H // 2)
    factor = freq[0] * waves.astype(F32) * (2.0 / H)
    return factor * factor


def cols_of(r):
    return pl.ds(pl.multiple_of(r * BLK, BLK), BLK)


def put_edges(place, inner, even_o, odd_o):
    low, high = slice(0, BAND), slice(ROWS - BAND, ROWS)
    side = lax.rem(place[1], 2)

    @pl.when(side == 0)
    def _():
        even_o[...] = inner[high]
        odd_o[...] = inner[low]

    @pl.when(side == 1)
    def _():
        even_o[...] = inner[low]
        odd_o[...] = inner[high]


def init_kernel(
    freq, place, count, load, stiff, mass, rows, pslot, normal, tangent, backward, cols,
    inner_o, even_o, odd_o, dyn_o, inv_o, hot_o, swap_o, listed_o, aux_o, backward_o, place_o, cols_o,
    s_buf, m_buf, l_buf, small_i, small_f, parts, sems,
):
    moves = [
        pltpu.make_async_copy(rows, small_i.at[0], sems.at[0]),
        pltpu.make_async_copy(pslot, small_i.at[1], sems.at[1]),
        pltpu.make_async_copy(normal, small_f.at[0], sems.at[2]),
        pltpu.make_async_copy(tangent, small_f.at[1], sems.at[3]),
        pltpu.make_async_copy(stiff.at[:, 0], s_buf, sems.at[4]),
        pltpu.make_async_copy(mass.at[:, 0], m_buf, sems.at[5]),
        pltpu.make_async_copy(load, l_buf, sems.at[6]),
        pltpu.make_async_copy(backward.at[place[0]], backward_o, sems.at[7]),
        pltpu.make_async_copy(cols, cols_o, sems.at[8]),
    ]
    for move in moves:
        move.start()
    factor = own_factor(freq, place)
    for move in moves[:4]:
        move.wait()
    in_block = lax.broadcasted_iota(jnp.int32, (BLK, CMAX), 0)
    wanted = small_i[0]
    for r in range(ROWS):
        hot_o[r * BLK : (r + 1) * BLK, :] = jnp.where(in_block + r * BLK == wanted, 1.0, 0.0).astype(BF16)
    swap_o[...] = jnp.where(
        lax.broadcasted_iota(jnp.int32, (CMAX, CMAX), 0) == small_i[1], 1.0, 0.0
    ).astype(BF16)
    live = lax.broadcasted_iota(jnp.int32, (1, CMAX), 1) < count[0]
    aux_o[RATIO : RATIO + 1, :] = small_f[1] / small_f[0]
    aux_o[LIMIT : LIMIT + 1, :] = jnp.where(live, small_f[0], 0.0)
    eye = lax.broadcasted_iota(jnp.int32, (BLK, BLK), 0) == lax.broadcasted_iota(
        jnp.int32, (BLK, BLK), 1
    )
    ones = jnp.ones((OWN, BLK), BF16)
    zero = jnp.zeros((BLK, BLK), BF16)
    for move in moves[4:7]:
        move.wait()
    for r in range(ROWS):
        s_diag = dot(ones, jnp.where(eye, s_buf[r], zero))
        m_diag = dot(ones, jnp.where(eye, m_buf[r], zero))
        dynamic = s_diag - factor * m_diag
        at = slice(r * BLK, (r + 1) * BLK)
        disp = l_buf[:, at] / dynamic
        dyn_o[:, at] = dynamic
        inv_o[:, at] = 1.0 / dynamic
        inner_o[r] = disp.astype(BF16)
        parts[: 3 * OWN, at] = split3(disp)
        parts[3 * OWN :, at] = split3(dynamic)
    listed = dot(parts[...], hot_o[...])
    listed_o[...] = sum3(listed[: 3 * OWN])
    aux_o[:OWN, :] = 1.0 / sum3(listed[3 * OWN :])
    put_edges(place, inner_o, even_o, odd_o)
    place_o[0] = place[0]
    place_o[1] = place[1]
    moves[7].wait()
    moves[8].wait()


def relative_kernel(own, far, swap, aux, _, out):
    facing = dot(split3(far[...]), swap[...])
    out[...] = (own[...] - sum3(facing)) * aux[RATIO : RATIO + 1, :]


INSIDE = tuple(range(BAND, ROWS - BAND))
OUTSIDE = tuple(range(BAND)) + tuple(range(ROWS - BAND, ROWS))


def product_kernel(*refs, edges, first, final, more):
    refs = list(refs)
    cols, freq, place, inner = refs[:4]
    del refs[:4]
    if edges:
        even, odd = refs[:2]
        del refs[:2]
    if first:
        stiff, mass = refs[:2]
        del refs[:2]
    else:
        wide = refs.pop(0)
    load, hot, scale = refs[:3]
    del refs[:3]
    if final:
        disp = refs.pop(0)
    if more:
        earlier = refs.pop(0)
    lin_o = refs.pop(0)
    if not final:
        listed_o = refs.pop(0)
    if first:
        wide = refs.pop(0)
    field, parts = refs
    own = place[1] * ROWS
    if edges:
        side = lax.rem(place[1], 2)
        far_end = BAND + ROWS
        field[BAND:far_end] = inner[...]
        field[pl.ds((1 - side) * far_end, BAND)] = even[...]
        field[pl.ds(side * far_end, BAND)] = odd[...]
        source, offset = field, own - BAND
    else:
        source, offset = inner, own
    factor = own_factor(freq, place)
    chosen = OUTSIDE if edges else INSIDE
    for i, r in enumerate(chosen):
        at = slice(r * BLK, (r + 1) * BLK)
        here = slice(i * BLK, (i + 1) * BLK)
        picked = [source[cols[s, r] - offset] for s in range(SLOTS)]
        if first:
            for s in range(SLOTS):
                wide[i, s * BLK : (s + 1) * BLK, :BLK] = stiff[r, s].T
                wide[i, s * BLK : (s + 1) * BLK, BLK:] = mass[r, s].T
        made = dot(jnp.concatenate(picked, axis=1), wide[i])
        applied = made[:, :BLK] - factor * made[:, BLK:]
        rounded = inner[r].astype(F32)
        if final:
            lin_o[:, here] = load[:, at] - (applied + scale[:, at] * (disp[:, at] - rounded))
        else:
            lin = rounded + (load[:, at] - applied) * scale[:, at]
            lin_o[:, here] = lin
            parts[:, here] = split3(lin)
    if not final:
        if edges:
            cut, tail = BAND * BLK, (ROWS - BAND) * BLK
            made = dot(parts[:, :cut], hot[:cut, :]) + dot(parts[:, cut:], hot[tail:, :])
        else:
            made = dot(parts[...], hot[BAND * BLK : (ROWS - BAND) * BLK, :])
        made = sum3(made)
        listed_o[...] = made + earlier[...] if more else made


def lin_block(inside, outside, r):
    if r in INSIDE:
        i = INSIDE.index(r)
        return inside[:, i * BLK : (i + 1) * BLK]
    i = OUTSIDE.index(r)
    return outside[:, i * BLK : (i + 1) * BLK]


def time_kernel(place, near, opposite, across, forward, backward, aux, *rest, final):
    rel = rest[-1]
    me = place[0]
    for ref, at, other in (
        (near, 0, 0), (near, 1, 2), (opposite, 0, 6), (opposite, 1, 4),
        (across, 0, 1), (across, 1, 3), (across, 2, 7), (across, 3, 5),
    ):
        to = pl.multiple_of(jnp.bitwise_xor(me, other) * OWN, OWN)
        rel[pl.ds(to, OWN), :] = ref[at * OWN : (at + 1) * OWN, :]
    whole = rel[...]
    high = whole.astype(BF16)
    low = (whole - high.astype(F32)).astype(BF16)
    stacked = jnp.concatenate([high, low, high], axis=0)
    step = 256
    total = jnp.zeros((2 * OWN, CMAX), F32)
    for n in range(0, TIME_POINTS, step):
        values = jnp.tanh(dot(forward[n : n + step, :], stacked)).astype(BF16)
        total = total + dot(backward[:, n : n + step], values)
    force = (total[:OWN] + total[OWN:]) * aux[LIMIT : LIMIT + 1, :]
    if final:
        rest[0][...] = force
        return
    lin_rows, force_o, listed_o, _ = rest
    force_o[...] = force
    listed_o[...] = lin_rows[...] - force * aux[:OWN, :]


def spread(force, hot_block):
    high = force.astype(BF16)
    low = (force - high.astype(F32)).astype(BF16)
    both = dot_nt(jnp.concatenate([high, low], axis=0), hot_block)
    return both[:OWN] + both[OWN:]


def update_kernel(place, force, hot, lin_a, lin_b, inv, inner_o, even_o, odd_o, *rest):
    add = force[...]
    for r in range(ROWS):
        at = slice(r * BLK, (r + 1) * BLK)
        lin = lin_block(lin_a, lin_b, r)
        disp = lin - spread(add, hot[at, :]) * inv[:, at]
        if rest:
            rest[0][:, at] = disp
        inner_o[r] = disp.astype(BF16)
    put_edges(place, inner_o, even_o, odd_o)


def finish_kernel(force, hot, lin_a, lin_b, inv, disp, disp_o, residual_o):
    add = force[...]
    for r in range(ROWS):
        at = slice(r * BLK, (r + 1) * BLK)
        lin = lin_block(lin_a, lin_b, r)
        residual = lin - spread(add, hot[at, :])
        residual_o[:, at] = residual
        disp_o[:, at] = disp[:, at] + residual * inv[:, at]


def shape(dims, dtype=F32):
    return jax.ShapeDtypeStruct(dims, dtype)


def held(dims, dtype=F32):
    return pltpu.VMEM(dims, dtype)


def params(limit=4):
    return pltpu.CompilerParams(vmem_limit_bytes=limit << 20)


def cost(us):
    return pl.CostEstimate(flops=int(us * 1.0e9), bytes_accessed=int(us * 3.0e6), transcendentals=0)


FULL = (OWN, DOFS)
PART = (OWN, HALF * BLK)
LIST = (OWN, CMAX)
EDGE = (BAND, OWN, BLK)
BLOCKED = (ROWS, OWN, BLK)
WIDE = (HALF, SLOTS * BLK, 2 * BLK)


def local(
    load,
    stiff_blocks,
    mass_blocks,
    block_cols,
    contact_rows,
    partner_slot,
    contact_count,
    normal_load,
    contact_stiffness,
    frequency,
):
    harm = lax.axis_index("harm").astype(jnp.int32)
    comp = lax.axis_index("comp").astype(jnp.int32)
    place = jnp.stack([harm, comp])
    groups = lax.axis_size("comp")
    devices = lax.axis_size("harm")
    cols = block_cols.T
    forward, backward = (jnp.asarray(t) for t in tables())
    inner, even, odd, dyn, inv, hot, swap, listed, aux, backward, place, cols = pl.pallas_call(
        init_kernel,
        out_shape=(
            shape(BLOCKED, BF16), shape(EDGE, BF16), shape(EDGE, BF16),
            shape(FULL), shape(FULL), shape((DOFS, CMAX), BF16), shape((CMAX, CMAX), BF16),
            shape(LIST), shape((32, CMAX)), shape((2 * OWN, TIME_POINTS), BF16),
            pltpu.SMEM((2,), jnp.int32), pltpu.SMEM((SLOTS, ROWS), jnp.int32),
        ),
        in_specs=[SM, SM, SM] + [FAR] * 9,
        out_specs=(VM,) * 10 + (SM,) * 2,
        scratch_shapes=[
            pltpu.VMEM((ROWS, BLK, BLK), BF16),
            pltpu.VMEM((ROWS, BLK, BLK), BF16),
            pltpu.VMEM(FULL, F32),
            pltpu.VMEM((2, 1, CMAX), jnp.int32),
            pltpu.VMEM((2, 1, CMAX), F32),
            pltpu.VMEM((6 * OWN, DOFS), BF16),
            pltpu.SemaphoreType.DMA((9,)),
        ],
        compiler_params=params(),
        cost_estimate=cost(3.0),
        name="init",
    )(
        frequency, place, contact_count, *(
            pltpu.with_memory_space_constraint(x, pltpu.HBM)
            for x in (load, stiff_blocks, mass_blocks, contact_rows, partner_slot, normal_load, contact_stiffness, backward, cols)
        )
    )

    stiff_late, mass_late, _ = lax.optimization_barrier((stiff_blocks, mass_blocks, listed))
    stiff_near = pltpu.with_memory_space_constraint(stiff_late, pltpu.VMEM)
    mass_near = pltpu.with_memory_space_constraint(mass_late, pltpu.VMEM)

    across = groups // 2
    far = [(i, i ^ across) for i in range(groups)]
    evens = [(i, i ^ 1) for i in range(groups)]
    odds = [(i, j) for i in range(groups) if 0 <= (j := i - 1 + 2 * (i % 2)) < groups]

    def flipped(x, bits):
        return lax.ppermute(x, "harm", [(i, i ^ bits) for i in range(devices)])

    wides = []
    for sweep in range(ITERS):
        first, final = sweep == 0, sweep == ITERS - 1
        own_far = lax.ppermute(listed, "comp", far)
        even_in = lax.ppermute(even, "comp", evens)
        odd_in = lax.ppermute(odd, "comp", odds)

        def product(edges, extra):
            take = [cols, frequency, place, inner] + ([even_in, odd_in] if edges else [])
            if first:
                take += [stiff_near, mass_near]
            else:
                take += [pltpu.with_memory_space_constraint(wides[int(edges)], pltpu.VMEM)]
            take += [load, hot, dyn if final else inv]
            take += ([kept] if final else []) + extra
            give = [shape(PART)] + ([] if final else [shape(LIST)]) + ([held(WIDE, BF16)] if first else [])
            outs = pl.pallas_call(
                functools.partial(product_kernel, edges=edges, first=first, final=final, more=bool(extra)),
                out_shape=tuple(give),
                in_specs=[SM] * 3 + [VM] * (len(take) - 3),
                out_specs=(VM,) * len(give),
                scratch_shapes=[
                    pltpu.VMEM((ROWS + 2 * BAND, OWN, BLK), BF16),
                    pltpu.VMEM((3 * OWN, HALF * BLK), BF16),
                ],
                compiler_params=params(),
                cost_estimate=cost(3.0 if first else 1.5),
                name="edges" if edges else "inside",
            )(*take)
            if first:
                wides.append(outs[-1])
            return outs[:1] if final else outs[:2]

        inside = product(False, [])
        relative = pl.pallas_call(
            relative_kernel,
            out_shape=shape(LIST),
            in_specs=[VM] * 5,
            out_specs=VM,
            compiler_params=params(),
            cost_estimate=cost(0.2),
            name="relative",
        )(listed, own_far, swap, aux, inside[0])
        near = jnp.concatenate([relative, flipped(relative, 2)], axis=0)
        opposite = flipped(near, 6)
        across_core = flipped(jnp.concatenate([near, opposite], axis=0), 1)
        outside = product(True, [] if final else [inside[1]])
        lins = [inside[0], outside[0]]
        timed = pl.pallas_call(
            functools.partial(time_kernel, final=final),
            out_shape=(shape(LIST),) * (1 if final else 2),
            in_specs=[SM] + [VM] * (6 if final else 7),
            out_specs=(VM,) * (1 if final else 2),
            scratch_shapes=[pltpu.VMEM((H, CMAX), F32)],
            compiler_params=params(),
            cost_estimate=cost(1.0),
            name="time",
        )(place, near, opposite, across_core, forward, backward, aux, *([] if final else [outside[1]]))
        if final:
            return pl.pallas_call(
                finish_kernel,
                out_shape=(shape(FULL), shape(FULL)),
                in_specs=[VM] * 6,
                out_specs=(VM, VM),
                compiler_params=params(),
                name="finish",
            )(timed[0], hot, *lins, inv, kept)
        force, listed = timed
        keep = (shape(FULL),) if sweep == ITERS - 2 else ()
        inner, even, odd, *rest = pl.pallas_call(
            update_kernel,
            out_shape=(shape(BLOCKED, BF16), shape(EDGE, BF16), shape(EDGE, BF16)) + keep,
            in_specs=[SM] + [VM] * 5,
            out_specs=(VM,) * (3 + len(keep)),
            compiler_params=params(),
            cost_estimate=cost(0.8),
            name="update",
        )(place, force, hot, *lins, inv)
        if rest:
            kept = rest[0]


def solution(mesh):
    placed = (
        P("harm", "comp"),
        P("comp", None, None, None),
        P("comp", None, None, None),
        P("comp", None),
        P("comp", None),
        P("comp", None),
        P("comp"),
        P("comp", None),
        P("comp", None),
        P(),
    )
    return jax.shard_map(
        local,
        mesh=mesh,
        in_specs=placed,
        out_specs=(P("harm", "comp"), P("harm", "comp")),
        check_vma=False,
    )
```

```python
import functools
import math

import jax
import jax.numpy as jnp
import ml_dtypes
import numpy as np
from jax import lax
from jax.experimental import pallas as pl
from jax.experimental.pallas import tpu as pltpu
from jax.sharding import PartitionSpec as P

H = 128
TIME_POINTS = 1024
BLK = 128
SLOTS = 8
BAND = 8
ITERS = 3
OWN = 16
ROWS = 32
HALF = ROWS // 2
INV = OWN
RATIO = 32
LIMIT = 33
FACING = 34
MINE = 48
CMAX = 256
DOFS = ROWS * BLK
F32 = jnp.float32
BF16 = jnp.bfloat16
LAST_LAST = (((1,), (1,)), ((), ()))

VM = pl.BlockSpec(memory_space=pltpu.VMEM)
SM = pl.BlockSpec(memory_space=pltpu.SMEM)
FAR = pl.BlockSpec(memory_space=pltpu.HBM)


def tables():
    j = np.arange(H)
    waves = np.where(j <= H // 2, j, j - H // 2)
    phase = (np.arange(TIME_POINTS)[:, None] * waves[None, :]) % TIME_POINTS
    angle = phase.astype(np.float64) * (2.0 * math.pi / TIME_POINTS)
    table = np.where(j[None, :] <= H // 2, np.cos(angle), np.sin(angle)).astype(np.float32)
    high = table.astype(ml_dtypes.bfloat16)
    low = (table - high.astype(np.float32)).astype(ml_dtypes.bfloat16)
    half = TIME_POINTS // 2
    forward = np.stack(
        [
            np.concatenate([high[:half, p::2], high[:half, p::2], low[:half, p::2]], axis=1)
            for p in range(2)
        ]
    )
    weights = (np.where(j == 0, 1.0, 2.0) / TIME_POINTS).astype(np.float32)
    back = (table * weights[None, :]).T
    back_high = back.astype(ml_dtypes.bfloat16)
    back_low = (back - back_high.astype(np.float32)).astype(ml_dtypes.bfloat16)
    order = np.arange(TIME_POINTS).reshape(2, -1, BLK).transpose(1, 0, 2).reshape(-1)
    back_high, back_low = back_high[:, order], back_low[:, order]
    backward = np.concatenate(
        [
            back_high.reshape(H // OWN, OWN, TIME_POINTS),
            back_low.reshape(H // OWN, OWN, TIME_POINTS),
        ],
        axis=1,
    )
    return forward, backward


def dot(a, b):
    return jnp.dot(a, b, preferred_element_type=F32)


def dot_nt(a, b):
    return lax.dot_general(a, b, LAST_LAST, preferred_element_type=F32)


def split3(x):
    high = x.astype(BF16)
    rest = x - high.astype(F32)
    mid = rest.astype(BF16)
    low = (rest - mid.astype(F32)).astype(BF16)
    return jnp.concatenate([high, mid, low], axis=0)


def sum3(y):
    n = y.shape[0] // 3
    return y[:n] + y[n : 2 * n] + y[2 * n :]


def own_factor(freq, place):
    j = place[0] * OWN + lax.broadcasted_iota(jnp.int32, (OWN, BLK), 0)
    waves = jnp.where(j <= H // 2, j, j - H // 2)
    factor = freq[0] * waves.astype(F32) * (2.0 / H)
    return factor * factor


def cols_of(r):
    return pl.ds(pl.multiple_of(r * BLK, BLK), BLK)


def put_edges(place, inner, even_o, odd_o):
    low, high = slice(0, BAND), slice(ROWS - BAND, ROWS)
    side = lax.rem(place[1], 2)

    @pl.when(side == 0)
    def _():
        even_o[...] = inner[high]
        odd_o[...] = inner[low]

    @pl.when(side == 1)
    def _():
        even_o[...] = inner[low]
        odd_o[...] = inner[high]


def one_hot(wanted):
    row = lax.broadcasted_iota(jnp.int32, (CMAX, CMAX), 0)
    return jnp.where(row == wanted, 1.0, 0.0).astype(BF16)


def init_kernel(
    freq, place, count, load, stiff, mass, rows, pslot, normal, tangent, backward, cols,
    inner_o, even_o, odd_o, dyn_o, inv_o, hot_o, swap_o, mine_o, backward_o, place_o, cols_o,
    s_buf, m_buf, l_buf, small_i, small_f, parts, sems,
):
    moves = [
        pltpu.make_async_copy(rows, small_i.at[0], sems.at[0]),
        pltpu.make_async_copy(pslot, small_i.at[1], sems.at[1]),
        pltpu.make_async_copy(normal, small_f.at[0], sems.at[2]),
        pltpu.make_async_copy(tangent, small_f.at[1], sems.at[3]),
        pltpu.make_async_copy(stiff.at[:, 0], s_buf, sems.at[4]),
        pltpu.make_async_copy(mass.at[:, 0], m_buf, sems.at[5]),
        pltpu.make_async_copy(load, l_buf, sems.at[6]),
        pltpu.make_async_copy(backward.at[place[0]], backward_o, sems.at[7]),
        pltpu.make_async_copy(cols, cols_o, sems.at[8]),
    ]
    for move in moves:
        move.start()
    factor = own_factor(freq, place)
    for move in moves[:4]:
        move.wait()
    in_block = lax.broadcasted_iota(jnp.int32, (BLK, CMAX), 0)
    wanted = small_i[0]
    for r in range(ROWS):
        hot_o[r * BLK : (r + 1) * BLK, :] = jnp.where(in_block + r * BLK == wanted, 1.0, 0.0).astype(BF16)
    swap_o[...] = one_hot(small_i[1])
    live = lax.broadcasted_iota(jnp.int32, (1, CMAX), 1) < count[0]
    mine_o[2 * OWN :, :] = jnp.zeros((MINE - 2 * OWN, CMAX), F32)
    mine_o[RATIO : RATIO + 1, :] = small_f[1] / small_f[0]
    mine_o[LIMIT : LIMIT + 1, :] = jnp.where(live, small_f[0], 0.0)
    mine_o[FACING : FACING + 1, :] = small_i[1].astype(F32)
    eye = lax.broadcasted_iota(jnp.int32, (BLK, BLK), 0) == lax.broadcasted_iota(
        jnp.int32, (BLK, BLK), 1
    )
    ones = jnp.ones((OWN, BLK), BF16)
    zero = jnp.zeros((BLK, BLK), BF16)
    for move in moves[4:7]:
        move.wait()
    for r in range(ROWS):
        s_diag = dot(ones, jnp.where(eye, s_buf[r], zero))
        m_diag = dot(ones, jnp.where(eye, m_buf[r], zero))
        dynamic = s_diag - factor * m_diag
        at = slice(r * BLK, (r + 1) * BLK)
        disp = l_buf[:, at] / dynamic
        dyn_o[:, at] = dynamic
        inv_o[:, at] = 1.0 / dynamic
        inner_o[r] = disp.astype(BF16)
        parts[: 3 * OWN, at] = split3(disp)
        parts[3 * OWN :, at] = split3(dynamic)
    listed = dot(parts[...], hot_o[...])
    mine_o[:OWN, :] = sum3(listed[: 3 * OWN])
    mine_o[INV : INV + OWN, :] = 1.0 / sum3(listed[3 * OWN :])
    put_edges(place, inner_o, even_o, odd_o)
    place_o[0] = place[0]
    place_o[1] = place[1]
    place_o[2] = place[2]
    moves[7].wait()
    moves[8].wait()


def relative_kernel(mine, far, swap, *refs, first, final):
    if first:
        out, swap_far = refs[-2:]
        wanted = far[FACING : FACING + 1, :].astype(jnp.int32)
        swap_far[...] = one_hot(wanted)
        near_disp, far_disp = mine[:OWN, :], far[:OWN, :]
    else:
        swap_far, force, near_lin, far_lin, out = refs
        near_disp = near_lin[...] - force[:, :CMAX] * mine[INV : INV + OWN, :]
        far_disp = far_lin[...] - force[:, CMAX:] * far[INV : INV + OWN, :]
    facing = sum3(dot(split3(far_disp), swap[...]))
    out[:, :CMAX] = (near_disp - facing) * mine[RATIO : RATIO + 1, :]
    if not final:
        facing = sum3(dot(split3(near_disp), swap_far[...]))
        out[:, CMAX:] = (far_disp - facing) * far[RATIO : RATIO + 1, :]


def join_kernel(a, b, *rest):
    out = rest[-1]
    n = a.shape[0]
    out[:n, :] = a[...]
    out[n:, :] = b[...]


INSIDE = tuple(range(BAND, ROWS - BAND))
OUTSIDE = tuple(range(BAND)) + tuple(range(ROWS - BAND, ROWS))


def product_kernel(*refs, edges, first, final, more, after):
    refs = list(refs)
    cols, freq, place, inner = refs[:4]
    del refs[:4]
    if edges:
        even, odd = refs[:2]
        del refs[:2]
    if first:
        stiff, mass = refs[:2]
        del refs[:2]
    else:
        wide = refs.pop(0)
    load, hot, scale = refs[:3]
    del refs[:3]
    if final:
        disp = refs.pop(0)
    if more:
        earlier = refs.pop(0)
    del refs[:after]
    lin_o = refs.pop(0)
    if not final:
        listed_o = refs.pop(0)
    if first:
        wide = refs.pop(0)
    field, parts = refs
    own = place[1] * ROWS
    if edges:
        side = lax.rem(place[1], 2)
        far_end = BAND + ROWS
        field[BAND:far_end] = inner[...]
        field[pl.ds((1 - side) * far_end, BAND)] = even[...]
        alone = (place[1] == 0) | (place[1] == place[2] - 1)
        field[pl.ds(side * far_end, BAND)] = jnp.where(alone, jnp.zeros(odd.shape, BF16), odd[...])
        source, offset = field, own - BAND
    else:
        source, offset = inner, own
    factor = own_factor(freq, place)
    chosen = OUTSIDE if edges else INSIDE
    for i, r in enumerate(chosen):
        at = slice(r * BLK, (r + 1) * BLK)
        here = slice(i * BLK, (i + 1) * BLK)
        picked = [source[cols[s, r] - offset] for s in range(SLOTS)]
        if first:
            for s in range(SLOTS):
                wide[i, s * BLK : (s + 1) * BLK, :BLK] = stiff[r, s].T
                wide[i, s * BLK : (s + 1) * BLK, BLK:] = mass[r, s].T
        made = dot(jnp.concatenate(picked, axis=1), wide[i])
        applied = made[:, :BLK] - factor * made[:, BLK:]
        rounded = inner[r].astype(F32)
        if final:
            lin_o[:, here] = load[:, at] - (applied + scale[:, at] * (disp[:, at] - rounded))
        else:
            lin = rounded + (load[:, at] - applied) * scale[:, at]
            lin_o[:, here] = lin
            parts[:, here] = split3(lin)
    if not final:
        if edges:
            cut, tail = BAND * BLK, (ROWS - BAND) * BLK
            made = dot(parts[:, :cut], hot[:cut, :]) + dot(parts[:, cut:], hot[tail:, :])
        else:
            made = dot(parts[...], hot[BAND * BLK : (ROWS - BAND) * BLK, :])
        made = sum3(made)
        listed_o[...] = made + earlier[...] if more else made


def lin_block(inside, outside, r):
    if r in INSIDE:
        i = INSIDE.index(r)
        return inside[:, i * BLK : (i + 1) * BLK]
    i = OUTSIDE.index(r)
    return outside[:, i * BLK : (i + 1) * BLK]


def time_kernel(place, near, opposite, across, forward, backward, mine, far, *rest, final):
    force_o, rel = rest[-2:]
    me, width = place[0], near.shape[1]
    for ref, at, other in (
        (near, 0, 0), (near, 1, 2), (opposite, 0, 6), (opposite, 1, 4),
        (across, 0, 1), (across, 1, 3), (across, 2, 7), (across, 3, 5),
    ):
        to = pl.multiple_of(jnp.bitwise_xor(me, other) * OWN, OWN)
        for c in range(width // BLK):
            rel[c, pl.ds(to, OWN), :] = ref[at * OWN : (at + 1) * OWN, c * BLK : (c + 1) * BLK]
    for first_col in range(0, width, CMAX):
        stacked = []
        for parity in range(2):
            part = jnp.concatenate(
                [rel[first_col // BLK + c, pl.ds(parity, H // 2, stride=2), :] for c in range(CMAX // BLK)], axis=1
            )
            high = part.astype(BF16)
            low = (part - high.astype(F32)).astype(BF16)
            stacked.append(jnp.concatenate([high, low, high], axis=0))
        total = jnp.zeros((2 * OWN, CMAX), F32)
        for n in range(0, TIME_POINTS // 2, BLK):
            even = dot(forward[0, n : n + BLK, :], stacked[0])
            odd = dot(forward[1, n : n + BLK, :], stacked[1])
            values = jnp.concatenate([jnp.tanh(even + odd).astype(BF16), jnp.tanh(even - odd).astype(BF16)], axis=0)
            total = total + dot(backward[:, 2 * n : 2 * n + 2 * BLK], values)
        limit = (far if first_col else mine)[LIMIT : LIMIT + 1, :]
        force_o[:, first_col : first_col + CMAX] = (total[:OWN] + total[OWN:]) * limit


def spread(force, hot_block):
    high = force.astype(BF16)
    low = (force - high.astype(F32)).astype(BF16)
    both = dot_nt(jnp.concatenate([high, low], axis=0), hot_block)
    return both[:OWN] + both[OWN:]


def update_kernel(place, force, hot, lin_a, lin_b, inv, inner_o, even_o, odd_o, *rest):
    add = force[:, :CMAX]
    for r in range(ROWS):
        at = slice(r * BLK, (r + 1) * BLK)
        lin = lin_block(lin_a, lin_b, r)
        disp = lin - spread(add, hot[at, :]) * inv[:, at]
        if rest:
            rest[0][:, at] = disp
        inner_o[r] = disp.astype(BF16)
    put_edges(place, inner_o, even_o, odd_o)


def finish_kernel(force, hot, lin_a, lin_b, inv, disp, disp_o, residual_o, disp_b, residual_b, sems):
    add = force[:, :CMAX]
    moves = []
    for r in range(ROWS):
        at = slice(r * BLK, (r + 1) * BLK)
        residual = lin_block(lin_a, lin_b, r) - spread(add, hot[at, :])
        residual_b[:, at] = residual
        disp_b[:, at] = disp[:, at] + residual * inv[:, at]
        if r % BAND == BAND - 1:
            part, ready = r // BAND, pl.ds((r + 1 - BAND) * BLK, BAND * BLK)
            moves.append(pltpu.make_async_copy(disp_b.at[:, ready], disp_o.at[:, ready], sems.at[0, part]))
            moves.append(pltpu.make_async_copy(residual_b.at[:, ready], residual_o.at[:, ready], sems.at[1, part]))
            for move in moves[-2:]:
                move.start()
    for move in moves:
        move.wait()


def shape(dims, dtype=F32):
    return jax.ShapeDtypeStruct(dims, dtype)


def held(dims, dtype=F32):
    return pltpu.VMEM(dims, dtype)


def params(limit=4):
    return pltpu.CompilerParams(vmem_limit_bytes=limit << 20)


def cost(us):
    return pl.CostEstimate(flops=int(us * 1.0e9), bytes_accessed=int(us * 3.0e6), transcendentals=0)


FULL = (OWN, DOFS)
PART = (OWN, HALF * BLK)
LIST = (OWN, CMAX)
EDGE = (BAND, OWN, BLK)
BLOCKED = (ROWS, OWN, BLK)
WIDE = (HALF, SLOTS * BLK, 2 * BLK)


def local(
    load,
    stiff_blocks,
    mass_blocks,
    block_cols,
    contact_rows,
    partner_slot,
    contact_count,
    normal_load,
    contact_stiffness,
    frequency,
):
    harm = lax.axis_index("harm").astype(jnp.int32)
    comp = lax.axis_index("comp").astype(jnp.int32)
    place = jnp.stack([harm, comp, jnp.int32(lax.axis_size("comp"))])
    groups = lax.axis_size("comp")
    devices = lax.axis_size("harm")
    cols = block_cols.T
    forward, backward = (jnp.asarray(t) for t in tables())
    inner, even, odd, dyn, inv, hot, swap, mine, backward, place, cols = pl.pallas_call(
        init_kernel,
        out_shape=(
            shape(BLOCKED, BF16), shape(EDGE, BF16), shape(EDGE, BF16),
            shape(FULL), shape(FULL), shape((DOFS, CMAX), BF16), shape((CMAX, CMAX), BF16),
            shape((MINE, CMAX)), shape((2 * OWN, TIME_POINTS), BF16),
            pltpu.SMEM((3,), jnp.int32), pltpu.SMEM((SLOTS, ROWS), jnp.int32),
        ),
        in_specs=[SM, SM, SM] + [FAR] * 9,
        out_specs=(VM,) * 9 + (SM,) * 2,
        scratch_shapes=[
            pltpu.VMEM((ROWS, BLK, BLK), BF16),
            pltpu.VMEM((ROWS, BLK, BLK), BF16),
            pltpu.VMEM(FULL, F32),
            pltpu.VMEM((2, 1, CMAX), jnp.int32),
            pltpu.VMEM((2, 1, CMAX), F32),
            pltpu.VMEM((6 * OWN, DOFS), BF16),
            pltpu.SemaphoreType.DMA((9,)),
        ],
        compiler_params=params(),
        cost_estimate=cost(3.0),
        name="init",
    )(
        frequency, place, contact_count, *(
            pltpu.with_memory_space_constraint(x, pltpu.HBM)
            for x in (load, stiff_blocks, mass_blocks, contact_rows, partner_slot, normal_load, contact_stiffness, backward, cols)
        )
    )

    stiff_late, mass_late, _ = lax.optimization_barrier((stiff_blocks, mass_blocks, mine))
    stiff_near = pltpu.with_memory_space_constraint(stiff_late, pltpu.VMEM)
    mass_near = pltpu.with_memory_space_constraint(mass_late, pltpu.VMEM)

    across = groups // 2
    facing = [(i, i ^ across) for i in range(groups)]
    evens = [(i, i ^ 1) for i in range(groups)]
    odds = [(i, (i - 1 + 2 * (i % 2)) % groups) for i in range(groups)]

    def flipped(x, bits):
        return lax.ppermute(x, "harm", [(i, i ^ bits) for i in range(devices)])

    far = lax.ppermute(mine, "comp", facing)
    def join(a, b, *after):
        return pl.pallas_call(
            join_kernel,
            out_shape=shape((2 * a.shape[0], a.shape[1])),
            in_specs=[VM] * (2 + len(after)),
            out_specs=VM,
            compiler_params=params(),
            cost_estimate=cost(0.1),
            name="join",
        )(a, b, *after)

    wides = {}
    for sweep in range(ITERS):
        first, final = sweep == 0, sweep == ITERS - 1
        even_in = lax.ppermute(even, "comp", evens)
        odd_in = lax.ppermute(odd, "comp", odds)

        def product(edges, extra, after=()):
            take = [cols, frequency, place, inner] + ([even_in, odd_in] if edges else [])
            if first:
                take += [stiff_near, mass_near]
            else:
                take += [pltpu.with_memory_space_constraint(wides[edges], pltpu.VMEM)]
            take += [load, hot, dyn if final else inv]
            take += ([kept] if final else []) + [*extra, *after]
            give = [shape(PART)] + ([] if final else [shape(LIST)]) + ([held(WIDE, BF16)] if first else [])
            outs = pl.pallas_call(
                functools.partial(
                    product_kernel, edges=edges, first=first, final=final, more=bool(extra), after=len(after)
                ),
                out_shape=tuple(give),
                in_specs=[SM] * 3 + [VM] * (len(take) - 3),
                out_specs=(VM,) * len(give),
                scratch_shapes=[
                    pltpu.VMEM((ROWS + 2 * BAND, OWN, BLK), BF16),
                    pltpu.VMEM((3 * OWN, HALF * BLK), BF16),
                ],
                compiler_params=params(),
                cost_estimate=cost(3.0 if first else 1.5),
                name="edges" if edges else "inside",
            )(*take)
            if first:
                wides[edges] = outs[-1]
            return outs[:1] if final else outs[:2]

        wide_list = LIST if final else (OWN, 2 * CMAX)
        given = [mine, far, swap] + ([even_in, odd_in] if first else [swap_far, force, near_lin, far_lin])
        made = pl.pallas_call(
            functools.partial(relative_kernel, first=first, final=final),
            out_shape=(shape(wide_list),) + ((shape((CMAX, CMAX), BF16),) if first else ()),
            in_specs=[VM] * len(given),
            out_specs=(VM,) * (2 if first else 1),
            compiler_params=params(),
            cost_estimate=cost(0.2),
            name="relative",
        )(*given)
        relative = made[0]
        if first:
            swap_far = made[1]
        beside = flipped(relative, 2)
        if first:
            outside = product(True, [])
            near = join(relative, beside, outside[0])
            inside = product(False, outside[1:], [near])
            added = inside
        else:
            near = join(relative, beside)
            inside = product(False, [], [near])
            outside = product(True, inside[1:])
            added = outside
        opposite = flipped(near, 6)
        across_core = flipped(join(near, opposite, inside[0], outside[0]), 1)
        lins = [inside[0], outside[0]]
        if not final:
            near_lin = added[1]
            far_lin = lax.ppermute(near_lin, "comp", facing)
        given = [near, opposite, across_core, forward, backward, mine, far]
        force = pl.pallas_call(
            functools.partial(time_kernel, final=final),
            out_shape=shape(wide_list),
            in_specs=[SM] + [VM] * len(given),
            out_specs=VM,
            scratch_shapes=[pltpu.VMEM((wide_list[1] // BLK, H, BLK), F32)],
            compiler_params=params(),
            cost_estimate=cost(1.0 if final else 1.8),
            name="time",
        )(place, *given)
        if final:
            return pl.pallas_call(
                finish_kernel,
                out_shape=(shape(FULL), shape(FULL)),
                in_specs=[VM] * 6,
                out_specs=(FAR, FAR),
                scratch_shapes=[
                    pltpu.VMEM(FULL, F32),
                    pltpu.VMEM(FULL, F32),
                    pltpu.SemaphoreType.DMA((2, ROWS // BAND)),
                ],
                compiler_params=params(),
                name="finish",
            )(force, hot, *lins, inv, kept)
        keep = (shape(FULL),) if sweep == ITERS - 2 else ()
        inner, even, odd, *rest = pl.pallas_call(
            update_kernel,
            out_shape=(shape(BLOCKED, BF16), shape(EDGE, BF16), shape(EDGE, BF16)) + keep,
            in_specs=[SM] + [VM] * 5,
            out_specs=(VM,) * (3 + len(keep)),
            compiler_params=params(),
            cost_estimate=cost(0.8),
            name="update",
        )(place, force, hot, *lins, inv)
        if rest:
            kept = rest[0]


def solution(mesh):
    placed = (
        P("harm", "comp"),
        P("comp", None, None, None),
        P("comp", None, None, None),
        P("comp", None),
        P("comp", None),
        P("comp", None),
        P("comp"),
        P("comp", None),
        P("comp", None),
        P(),
    )
    return jax.shard_map(
        local,
        mesh=mesh,
        in_specs=placed,
        out_specs=(P("harm", "comp"), P("harm", "comp")),
        check_vma=False,
    )
```

```python
import functools
import math

import jax
import jax.numpy as jnp
import ml_dtypes
import numpy as np
from jax import lax
from jax.experimental import pallas as pl
from jax.experimental.pallas import tpu as pltpu
from jax.sharding import PartitionSpec as P

H = 128
TIME_POINTS = 1024
BLK = 128
SLOTS = 8
BAND = 8
ITERS = 3
OWN = 16
ROWS = 32
HALF = ROWS // 2
INV = OWN
RATIO = 32
LIMIT = 33
FACING = 34
MINE = 48
CMAX = 256
DOFS = ROWS * BLK
F32 = jnp.float32
BF16 = jnp.bfloat16
LAST_LAST = (((1,), (1,)), ((), ()))

VM = pl.BlockSpec(memory_space=pltpu.VMEM)
SM = pl.BlockSpec(memory_space=pltpu.SMEM)
FAR = pl.BlockSpec(memory_space=pltpu.HBM)


def tables():
    j = np.arange(H)
    waves = np.where(j <= H // 2, j, j - H // 2)
    phase = (np.arange(TIME_POINTS)[:, None] * waves[None, :]) % TIME_POINTS
    angle = phase.astype(np.float64) * (2.0 * math.pi / TIME_POINTS)
    table = np.where(j[None, :] <= H // 2, np.cos(angle), np.sin(angle)).astype(np.float32)
    high = table.astype(ml_dtypes.bfloat16)
    low = (table - high.astype(np.float32)).astype(ml_dtypes.bfloat16)
    half = TIME_POINTS // 2
    forward = np.stack(
        [
            np.concatenate([high[:half, p::2], high[:half, p::2], low[:half, p::2]], axis=1)
            for p in range(2)
        ]
    )
    weights = (np.where(j == 0, 1.0, 2.0) / TIME_POINTS).astype(np.float32)
    back = (table * weights[None, :]).T
    back_high = back.astype(ml_dtypes.bfloat16)
    back_low = (back - back_high.astype(np.float32)).astype(ml_dtypes.bfloat16)
    order = np.arange(TIME_POINTS).reshape(2, -1, BLK).transpose(1, 0, 2).reshape(-1)
    back_high, back_low = back_high[:, order], back_low[:, order]
    backward = np.concatenate(
        [
            back_high.reshape(H // OWN, OWN, TIME_POINTS),
            back_low.reshape(H // OWN, OWN, TIME_POINTS),
        ],
        axis=1,
    )
    return forward, backward


def dot(a, b):
    return jnp.dot(a, b, preferred_element_type=F32)


def dot_nt(a, b):
    return lax.dot_general(a, b, LAST_LAST, preferred_element_type=F32)


def split3(x):
    high = x.astype(BF16)
    rest = x - high.astype(F32)
    mid = rest.astype(BF16)
    low = (rest - mid.astype(F32)).astype(BF16)
    return jnp.concatenate([high, mid, low], axis=0)


def sum3(y):
    n = y.shape[0] // 3
    return y[:n] + y[n : 2 * n] + y[2 * n :]


def own_factor(freq, place):
    j = place[0] * OWN + lax.broadcasted_iota(jnp.int32, (OWN, BLK), 0)
    waves = jnp.where(j <= H // 2, j, j - H // 2)
    factor = freq[0] * waves.astype(F32) * (2.0 / H)
    return factor * factor


def cols_of(r):
    return pl.ds(pl.multiple_of(r * BLK, BLK), BLK)


def put_edges(place, inner, even_o, odd_o):
    low, high = slice(0, BAND), slice(ROWS - BAND, ROWS)
    side = lax.rem(place[1], 2)

    @pl.when(side == 0)
    def _():
        even_o[...] = inner[high]
        odd_o[...] = inner[low]

    @pl.when(side == 1)
    def _():
        even_o[...] = inner[low]
        odd_o[...] = inner[high]


def one_hot(wanted):
    row = lax.broadcasted_iota(jnp.int32, (CMAX, CMAX), 0)
    return jnp.where(row == wanted, 1.0, 0.0).astype(BF16)


def init_kernel(
    freq, place, count, load, stiff, mass, rows, pslot, normal, tangent, backward, cols,
    inner_o, even_o, odd_o, dyn_o, inv_o, hot_o, swap_o, mine_o, backward_o, place_o, cols_o,
    s_buf, m_buf, l_buf, small_i, small_f, parts, sems,
):
    moves = [
        pltpu.make_async_copy(rows, small_i.at[0], sems.at[0]),
        pltpu.make_async_copy(pslot, small_i.at[1], sems.at[1]),
        pltpu.make_async_copy(normal, small_f.at[0], sems.at[2]),
        pltpu.make_async_copy(tangent, small_f.at[1], sems.at[3]),
        pltpu.make_async_copy(stiff.at[:, 0], s_buf, sems.at[4]),
        pltpu.make_async_copy(mass.at[:, 0], m_buf, sems.at[5]),
        pltpu.make_async_copy(load, l_buf, sems.at[6]),
        pltpu.make_async_copy(backward.at[place[0]], backward_o, sems.at[7]),
        pltpu.make_async_copy(cols, cols_o, sems.at[8]),
    ]
    for move in moves:
        move.start()
    factor = own_factor(freq, place)
    for move in moves[:4]:
        move.wait()
    in_block = lax.broadcasted_iota(jnp.int32, (BLK, CMAX), 0)
    wanted = small_i[0]
    for r in range(ROWS):
        hot_o[r * BLK : (r + 1) * BLK, :] = jnp.where(in_block + r * BLK == wanted, 1.0, 0.0).astype(BF16)
    swap_o[...] = one_hot(small_i[1])
    live = lax.broadcasted_iota(jnp.int32, (1, CMAX), 1) < count[0]
    mine_o[2 * OWN :, :] = jnp.zeros((MINE - 2 * OWN, CMAX), F32)
    mine_o[RATIO : RATIO + 1, :] = small_f[1] / small_f[0]
    mine_o[LIMIT : LIMIT + 1, :] = jnp.where(live, small_f[0], 0.0)
    mine_o[FACING : FACING + 1, :] = small_i[1].astype(F32)
    eye = lax.broadcasted_iota(jnp.int32, (BLK, BLK), 0) == lax.broadcasted_iota(
        jnp.int32, (BLK, BLK), 1
    )
    ones = jnp.ones((OWN, BLK), BF16)
    zero = jnp.zeros((BLK, BLK), BF16)
    for move in moves[4:7]:
        move.wait()
    for r in range(ROWS):
        s_diag = dot(ones, jnp.where(eye, s_buf[r], zero))
        m_diag = dot(ones, jnp.where(eye, m_buf[r], zero))
        dynamic = s_diag - factor * m_diag
        at = slice(r * BLK, (r + 1) * BLK)
        inverse = 1.0 / dynamic
        disp = l_buf[:, at] * inverse
        dyn_o[:, at] = dynamic
        inv_o[:, at] = inverse
        inner_o[r] = disp.astype(BF16)
        parts[: 3 * OWN, at] = split3(disp)
        parts[3 * OWN :, at] = split3(dynamic)
    listed = dot(parts[...], hot_o[...])
    mine_o[:OWN, :] = sum3(listed[: 3 * OWN])
    mine_o[INV : INV + OWN, :] = 1.0 / sum3(listed[3 * OWN :])
    put_edges(place, inner_o, even_o, odd_o)
    place_o[0] = place[0]
    place_o[1] = place[1]
    place_o[2] = place[2]
    moves[7].wait()
    moves[8].wait()


def relative_kernel(mine, far, swap, *refs, first, final):
    if first:
        out, swap_far = refs[-2:]
        wanted = far[FACING : FACING + 1, :].astype(jnp.int32)
        swap_far[...] = one_hot(wanted)
        near_disp, far_disp = mine[:OWN, :], far[:OWN, :]
    else:
        swap_far, force, near_lin, far_lin, _, out = refs
        near_disp = near_lin[...] - force[:, :CMAX] * mine[INV : INV + OWN, :]
        far_disp = far_lin[...] - force[:, CMAX:] * far[INV : INV + OWN, :]
    facing = sum3(dot(split3(far_disp), swap[...]))
    out[:, :CMAX] = (near_disp - facing) * mine[RATIO : RATIO + 1, :]
    if not final:
        facing = sum3(dot(split3(near_disp), swap_far[...]))
        out[:, CMAX:] = (far_disp - facing) * far[RATIO : RATIO + 1, :]


def join_kernel(a, b, *rest):
    out = rest[-1]
    n = a.shape[0]
    out[:n, :] = a[...]
    out[n:, :] = b[...]


INSIDE = tuple(range(BAND, ROWS - BAND))
OUTSIDE = tuple(range(BAND)) + tuple(range(ROWS - BAND, ROWS))


def product_kernel(*refs, edges, first, final, more, after):
    refs = list(refs)
    cols, freq, place, inner = refs[:4]
    del refs[:4]
    if edges:
        even, odd = refs[:2]
        del refs[:2]
    if first:
        stiff, mass = refs[:2]
        del refs[:2]
    else:
        wide = refs.pop(0)
    load, hot, scale = refs[:3]
    del refs[:3]
    if final:
        disp = refs.pop(0)
    if more:
        earlier = refs.pop(0)
    del refs[:after]
    lin_o = refs.pop(0)
    if not final:
        listed_o = refs.pop(0)
    if first:
        wide = refs.pop(0)
    field, parts = refs
    own = place[1] * ROWS
    if edges:
        side = lax.rem(place[1], 2)
        far_end = BAND + ROWS
        field[BAND:far_end] = inner[...]
        field[pl.ds((1 - side) * far_end, BAND)] = even[...]
        alone = (place[1] == 0) | (place[1] == place[2] - 1)
        field[pl.ds(side * far_end, BAND)] = jnp.where(alone, jnp.zeros(odd.shape, BF16), odd[...])
        source, offset = field, own - BAND
    else:
        source, offset = inner, own
    factor = own_factor(freq, place)
    chosen = OUTSIDE if edges else INSIDE
    for i, r in enumerate(chosen):
        at = slice(r * BLK, (r + 1) * BLK)
        here = slice(i * BLK, (i + 1) * BLK)
        picked = [source[cols[s, r] - offset] for s in range(SLOTS)]
        if first:
            for s in range(SLOTS):
                wide[i, s * BLK : (s + 1) * BLK, :BLK] = stiff[r, s].T
                wide[i, s * BLK : (s + 1) * BLK, BLK:] = mass[r, s].T
        made = dot(jnp.concatenate(picked, axis=1), wide[i])
        applied = made[:, :BLK] - factor * made[:, BLK:]
        rounded = inner[r].astype(F32)
        if final:
            lin_o[:, here] = load[:, at] - (applied + scale[:, at] * (disp[:, at] - rounded))
        else:
            lin = rounded + (load[:, at] - applied) * scale[:, at]
            lin_o[:, here] = lin
            parts[:, here] = split3(lin)
    if not final:
        if edges:
            cut, tail = BAND * BLK, (ROWS - BAND) * BLK
            made = dot(parts[:, :cut], hot[:cut, :]) + dot(parts[:, cut:], hot[tail:, :])
        else:
            made = dot(parts[...], hot[BAND * BLK : (ROWS - BAND) * BLK, :])
        made = sum3(made)
        listed_o[...] = made + earlier[...] if more else made


def lin_block(inside, outside, r):
    if r in INSIDE:
        i = INSIDE.index(r)
        return inside[:, i * BLK : (i + 1) * BLK]
    i = OUTSIDE.index(r)
    return outside[:, i * BLK : (i + 1) * BLK]


def time_kernel(place, near, opposite, across, forward, backward, mine, far, *rest, final):
    force_o, rel = rest[-2:]
    me, width = place[0], near.shape[1]
    for ref, at, other in (
        (near, 0, 0), (near, 1, 2), (opposite, 0, 6), (opposite, 1, 4),
        (across, 0, 1), (across, 1, 3), (across, 2, 7), (across, 3, 5),
    ):
        to = pl.multiple_of(jnp.bitwise_xor(me, other) * OWN, OWN)
        for c in range(width // BLK):
            rel[c, pl.ds(to, OWN), :] = ref[at * OWN : (at + 1) * OWN, c * BLK : (c + 1) * BLK]
    for first_col in range(0, width, CMAX):
        stacked = []
        for parity in range(2):
            part = jnp.concatenate(
                [rel[first_col // BLK + c, pl.ds(parity, H // 2, stride=2), :] for c in range(CMAX // BLK)], axis=1
            )
            high = part.astype(BF16)
            low = (part - high.astype(F32)).astype(BF16)
            stacked.append(jnp.concatenate([high, low, high], axis=0))
        total = jnp.zeros((2 * OWN, CMAX), F32)
        for n in range(0, TIME_POINTS // 2, BLK):
            even = dot(forward[0, n : n + BLK, :], stacked[0])
            odd = dot(forward[1, n : n + BLK, :], stacked[1])
            values = jnp.concatenate([jnp.tanh(even + odd).astype(BF16), jnp.tanh(even - odd).astype(BF16)], axis=0)
            total = total + dot(backward[:, 2 * n : 2 * n + 2 * BLK], values)
        limit = (far if first_col else mine)[LIMIT : LIMIT + 1, :]
        force_o[:, first_col : first_col + CMAX] = (total[:OWN] + total[OWN:]) * limit


def spread(force, hot_block):
    high = force.astype(BF16)
    low = (force - high.astype(F32)).astype(BF16)
    both = dot_nt(jnp.concatenate([high, low], axis=0), hot_block)
    return both[:OWN] + both[OWN:]


def update_kernel(place, force, hot, lin_a, lin_b, inv, inner_o, even_o, odd_o, *rest):
    add = force[:, :CMAX]
    for r in range(ROWS):
        at = slice(r * BLK, (r + 1) * BLK)
        lin = lin_block(lin_a, lin_b, r)
        disp = lin - spread(add, hot[at, :]) * inv[:, at]
        if rest:
            rest[0][:, at] = disp
        inner_o[r] = disp.astype(BF16)
    put_edges(place, inner_o, even_o, odd_o)


def finish_kernel(force, hot, lin_a, lin_b, inv, disp, disp_o, residual_o, disp_b, residual_b, sems):
    add = force[:, :CMAX]
    moves = []
    for r in range(ROWS):
        at = slice(r * BLK, (r + 1) * BLK)
        residual = lin_block(lin_a, lin_b, r) - spread(add, hot[at, :])
        residual_b[:, at] = residual
        disp_b[:, at] = disp[:, at] + residual * inv[:, at]
        if r % BAND == BAND - 1:
            part, ready = r // BAND, pl.ds((r + 1 - BAND) * BLK, BAND * BLK)
            moves.append(pltpu.make_async_copy(disp_b.at[:, ready], disp_o.at[:, ready], sems.at[0, part]))
            moves.append(pltpu.make_async_copy(residual_b.at[:, ready], residual_o.at[:, ready], sems.at[1, part]))
            for move in moves[-2:]:
                move.start()
    for move in moves:
        move.wait()


def shape(dims, dtype=F32):
    return jax.ShapeDtypeStruct(dims, dtype)


def held(dims, dtype=F32):
    return pltpu.VMEM(dims, dtype)


def params(limit=4):
    return pltpu.CompilerParams(vmem_limit_bytes=limit << 20)


def cost(us):
    return pl.CostEstimate(flops=int(us * 1.0e9), bytes_accessed=int(us * 3.0e6), transcendentals=0)


FULL = (OWN, DOFS)
PART = (OWN, HALF * BLK)
LIST = (OWN, CMAX)
EDGE = (BAND, OWN, BLK)
BLOCKED = (ROWS, OWN, BLK)
WIDE = (HALF, SLOTS * BLK, 2 * BLK)


def local(
    load,
    stiff_blocks,
    mass_blocks,
    block_cols,
    contact_rows,
    partner_slot,
    contact_count,
    normal_load,
    contact_stiffness,
    frequency,
):
    harm = lax.axis_index("harm").astype(jnp.int32)
    comp = lax.axis_index("comp").astype(jnp.int32)
    place = jnp.stack([harm, comp, jnp.int32(lax.axis_size("comp"))])
    groups = lax.axis_size("comp")
    devices = lax.axis_size("harm")
    cols = block_cols.T
    forward, backward = (jnp.asarray(t) for t in tables())
    inner, even, odd, dyn, inv, hot, swap, mine, backward, place, cols = pl.pallas_call(
        init_kernel,
        out_shape=(
            shape(BLOCKED, BF16), shape(EDGE, BF16), shape(EDGE, BF16),
            shape(FULL), shape(FULL), shape((DOFS, CMAX), BF16), shape((CMAX, CMAX), BF16),
            shape((MINE, CMAX)), shape((2 * OWN, TIME_POINTS), BF16),
            pltpu.SMEM((3,), jnp.int32), pltpu.SMEM((SLOTS, ROWS), jnp.int32),
        ),
        in_specs=[SM, SM, SM] + [FAR] * 9,
        out_specs=(VM,) * 9 + (SM,) * 2,
        scratch_shapes=[
            pltpu.VMEM((ROWS, BLK, BLK), BF16),
            pltpu.VMEM((ROWS, BLK, BLK), BF16),
            pltpu.VMEM(FULL, F32),
            pltpu.VMEM((2, 1, CMAX), jnp.int32),
            pltpu.VMEM((2, 1, CMAX), F32),
            pltpu.VMEM((6 * OWN, DOFS), BF16),
            pltpu.SemaphoreType.DMA((9,)),
        ],
        compiler_params=params(),
        cost_estimate=cost(3.0),
        name="init",
    )(
        frequency, place, contact_count, *(
            pltpu.with_memory_space_constraint(x, pltpu.HBM)
            for x in (load, stiff_blocks, mass_blocks, contact_rows, partner_slot, normal_load, contact_stiffness, backward, cols)
        )
    )

    stiff_late, mass_late, _ = lax.optimization_barrier((stiff_blocks, mass_blocks, mine))
    stiff_near = pltpu.with_memory_space_constraint(stiff_late, pltpu.VMEM)
    mass_near = pltpu.with_memory_space_constraint(mass_late, pltpu.VMEM)

    across = groups // 2
    facing = [(i, i ^ across) for i in range(groups)]
    evens = [(i, i ^ 1) for i in range(groups)]
    odds = [(i, (i - 1 + 2 * (i % 2)) % groups) for i in range(groups)]

    def flipped(x, bits):
        return lax.ppermute(x, "harm", [(i, i ^ bits) for i in range(devices)])

    far = lax.ppermute(mine, "comp", facing)
    def join(a, b, *after):
        return pl.pallas_call(
            join_kernel,
            out_shape=shape((2 * a.shape[0], a.shape[1])),
            in_specs=[VM] * (2 + len(after)),
            out_specs=VM,
            compiler_params=params(),
            cost_estimate=cost(0.1),
            name="join",
        )(a, b, *after)

    wides = {}
    for sweep in range(ITERS):
        first, final = sweep == 0, sweep == ITERS - 1
        even_in = lax.ppermute(even, "comp", evens)
        odd_in = lax.ppermute(odd, "comp", odds)

        def product(edges, extra, after=()):
            take = [cols, frequency, place, inner] + ([even_in, odd_in] if edges else [])
            if first:
                take += [stiff_near, mass_near]
            else:
                take += [pltpu.with_memory_space_constraint(wides[edges], pltpu.VMEM)]
            take += [load, hot, dyn if final else inv]
            take += ([kept] if final else []) + [*extra, *after]
            give = [shape(PART)] + ([] if final else [shape(LIST)]) + ([held(WIDE, BF16)] if first else [])
            outs = pl.pallas_call(
                functools.partial(
                    product_kernel, edges=edges, first=first, final=final, more=bool(extra), after=len(after)
                ),
                out_shape=tuple(give),
                in_specs=[SM] * 3 + [VM] * (len(take) - 3),
                out_specs=(VM,) * len(give),
                scratch_shapes=[
                    pltpu.VMEM((ROWS + 2 * BAND, OWN, BLK), BF16),
                    pltpu.VMEM((3 * OWN, HALF * BLK), BF16),
                ],
                compiler_params=params(),
                cost_estimate=cost(3.0 if first else 1.5),
                name="edges" if edges else "inside",
            )(*take)
            if first:
                wides[edges] = outs[-1]
            return outs[:1] if final else outs[:2]

        wide_list = LIST if final else (OWN, 2 * CMAX)
        given = [mine, far, swap] + ([even_in] if first else [swap_far, force, near_lin, far_lin, inner])
        made = pl.pallas_call(
            functools.partial(relative_kernel, first=first, final=final),
            out_shape=(shape(wide_list),) + ((shape((CMAX, CMAX), BF16),) if first else ()),
            in_specs=[VM] * len(given),
            out_specs=(VM,) * (2 if first else 1),
            compiler_params=params(),
            cost_estimate=cost(0.2),
            name="relative",
        )(*given)
        relative = made[0]
        if first:
            swap_far = made[1]
        beside = flipped(relative, 2)
        if first:
            inside = product(False, [])
            near = join(relative, beside, inside[0])
            outside = product(True, inside[1:], [near])
        else:
            near = join(relative, beside)
            inside = product(False, [], [near])
            outside = product(True, inside[1:])
        added = outside
        opposite = flipped(near, 6)
        across_core = flipped(join(near, opposite, inside[0], outside[0]), 1)
        lins = [inside[0], outside[0]]
        if not final:
            near_lin = added[1]
            far_lin = lax.ppermute(near_lin, "comp", facing)
        given = [near, opposite, across_core, forward, backward, mine, far]
        force = pl.pallas_call(
            functools.partial(time_kernel, final=final),
            out_shape=shape(wide_list),
            in_specs=[SM] + [VM] * len(given),
            out_specs=VM,
            scratch_shapes=[pltpu.VMEM((wide_list[1] // BLK, H, BLK), F32)],
            compiler_params=params(),
            cost_estimate=cost(0.01),
            name="time",
        )(place, *given)
        if final:
            return pl.pallas_call(
                finish_kernel,
                out_shape=(shape(FULL), shape(FULL)),
                in_specs=[VM] * 6,
                out_specs=(FAR, FAR),
                scratch_shapes=[
                    pltpu.VMEM(FULL, F32),
                    pltpu.VMEM(FULL, F32),
                    pltpu.SemaphoreType.DMA((2, ROWS // BAND)),
                ],
                compiler_params=params(),
                name="finish",
            )(force, hot, *lins, inv, kept)
        keep = (shape(FULL),) if sweep == ITERS - 2 else ()
        inner, even, odd, *rest = pl.pallas_call(
            update_kernel,
            out_shape=(shape(BLOCKED, BF16), shape(EDGE, BF16), shape(EDGE, BF16)) + keep,
            in_specs=[SM] + [VM] * 5,
            out_specs=(VM,) * (3 + len(keep)),
            compiler_params=params(),
            cost_estimate=cost(0.01),
            name="update",
        )(place, force, hot, *lins, inv)
        if rest:
            kept = rest[0]


def solution(mesh):
    placed = (
        P("harm", "comp"),
        P("comp", None, None, None),
        P("comp", None, None, None),
        P("comp", None),
        P("comp", None),
        P("comp", None),
        P("comp"),
        P("comp", None),
        P("comp", None),
        P(),
    )
    return jax.shard_map(
        local,
        mesh=mesh,
        in_specs=placed,
        out_specs=(P("harm", "comp"), P("harm", "comp")),
        check_vma=False,
    )
```

```python
import functools
import math

import jax
import jax.numpy as jnp
import ml_dtypes
import numpy as np
from jax import lax
from jax.experimental import pallas as pl
from jax.experimental.pallas import tpu as pltpu
from jax.sharding import PartitionSpec as P

H = 128
TIME_POINTS = 1024
BLK = 128
SLOTS = 8
BAND = 8
ITERS = 3
OWN = 16
ROWS = 32
HALF = ROWS // 2
INV = OWN
RATIO = 32
LIMIT = 33
FACING = 34
MINE = 48
CMAX = 256
DOFS = ROWS * BLK
F32 = jnp.float32
BF16 = jnp.bfloat16
LAST_LAST = (((1,), (1,)), ((), ()))

VM = pl.BlockSpec(memory_space=pltpu.VMEM)
SM = pl.BlockSpec(memory_space=pltpu.SMEM)
FAR = pl.BlockSpec(memory_space=pltpu.HBM)


def tables():
    j = np.arange(H)
    waves = np.where(j <= H // 2, j, j - H // 2)
    phase = (np.arange(TIME_POINTS)[:, None] * waves[None, :]) % TIME_POINTS
    angle = phase.astype(np.float64) * (2.0 * math.pi / TIME_POINTS)
    table = np.where(j[None, :] <= H // 2, np.cos(angle), np.sin(angle)).astype(np.float32)
    high = table.astype(ml_dtypes.bfloat16)
    low = (table - high.astype(np.float32)).astype(ml_dtypes.bfloat16)
    half = TIME_POINTS // 2
    forward = np.stack(
        [
            np.concatenate([high[:half, p::2], high[:half, p::2], low[:half, p::2]], axis=1)
            for p in range(2)
        ]
    )
    weights = (np.where(j == 0, 1.0, 2.0) / TIME_POINTS).astype(np.float32)
    back = (table * weights[None, :]).T
    back_high = back.astype(ml_dtypes.bfloat16)
    back_low = (back - back_high.astype(np.float32)).astype(ml_dtypes.bfloat16)
    order = np.arange(TIME_POINTS).reshape(2, -1, BLK).transpose(1, 0, 2).reshape(-1)
    back_high, back_low = back_high[:, order], back_low[:, order]
    backward = np.concatenate(
        [
            back_high.reshape(H // OWN, OWN, TIME_POINTS),
            back_low.reshape(H // OWN, OWN, TIME_POINTS),
        ],
        axis=1,
    )
    return forward, backward


def dot(a, b):
    return jnp.dot(a, b, preferred_element_type=F32)


def dot_nt(a, b):
    return lax.dot_general(a, b, LAST_LAST, preferred_element_type=F32)


def split3(x):
    high = x.astype(BF16)
    rest = x - high.astype(F32)
    mid = rest.astype(BF16)
    low = (rest - mid.astype(F32)).astype(BF16)
    return jnp.concatenate([high, mid, low], axis=0)


def sum3(y):
    n = y.shape[0] // 3
    return y[:n] + y[n : 2 * n] + y[2 * n :]


def own_factor(freq, place):
    j = place[0] * OWN + lax.broadcasted_iota(jnp.int32, (OWN, BLK), 0)
    waves = jnp.where(j <= H // 2, j, j - H // 2)
    factor = freq[0] * waves.astype(F32) * (2.0 / H)
    return factor * factor


def cols_of(r):
    return pl.ds(pl.multiple_of(r * BLK, BLK), BLK)


def put_edges(place, inner, even_o, odd_o):
    low, high = slice(0, BAND), slice(ROWS - BAND, ROWS)
    side = lax.rem(place[1], 2)

    @pl.when(side == 0)
    def _():
        even_o[...] = inner[high]
        odd_o[...] = inner[low]

    @pl.when(side == 1)
    def _():
        even_o[...] = inner[low]
        odd_o[...] = inner[high]


def one_hot(wanted):
    row = lax.broadcasted_iota(jnp.int32, (CMAX, CMAX), 0)
    return jnp.where(row == wanted, 1.0, 0.0).astype(BF16)


def init_kernel(
    freq, place, count, load, stiff, mass, rows, pslot, normal, tangent, backward, cols,
    inner_o, even_o, odd_o, dyn_o, inv_o, hot_o, swap_o, mine_o, backward_o, place_o, cols_o,
    s_buf, m_buf, l_buf, small_i, small_f, parts, sems,
):
    moves = [
        pltpu.make_async_copy(rows, small_i.at[0], sems.at[0]),
        pltpu.make_async_copy(pslot, small_i.at[1], sems.at[1]),
        pltpu.make_async_copy(normal, small_f.at[0], sems.at[2]),
        pltpu.make_async_copy(tangent, small_f.at[1], sems.at[3]),
        pltpu.make_async_copy(stiff.at[:, 0], s_buf, sems.at[4]),
        pltpu.make_async_copy(mass.at[:, 0], m_buf, sems.at[5]),
        pltpu.make_async_copy(load, l_buf, sems.at[6]),
        pltpu.make_async_copy(backward.at[place[0]], backward_o, sems.at[7]),
        pltpu.make_async_copy(cols, cols_o, sems.at[8]),
    ]
    for move in moves:
        move.start()
    factor = own_factor(freq, place)
    for move in moves[:4]:
        move.wait()
    in_block = lax.broadcasted_iota(jnp.int32, (BLK, CMAX), 0)
    wanted = small_i[0]
    for r in range(ROWS):
        hot_o[r * BLK : (r + 1) * BLK, :] = jnp.where(in_block + r * BLK == wanted, 1.0, 0.0).astype(BF16)
    swap_o[...] = one_hot(small_i[1])
    live = lax.broadcasted_iota(jnp.int32, (1, CMAX), 1) < count[0]
    mine_o[2 * OWN :, :] = jnp.zeros((MINE - 2 * OWN, CMAX), F32)
    mine_o[RATIO : RATIO + 1, :] = small_f[1] / small_f[0]
    mine_o[LIMIT : LIMIT + 1, :] = jnp.where(live, small_f[0], 0.0)
    mine_o[FACING : FACING + 1, :] = small_i[1].astype(F32)
    eye = lax.broadcasted_iota(jnp.int32, (BLK, BLK), 0) == lax.broadcasted_iota(
        jnp.int32, (BLK, BLK), 1
    )
    ones = jnp.ones((OWN, BLK), BF16)
    zero = jnp.zeros((BLK, BLK), BF16)
    for move in moves[4:7]:
        move.wait()
    for r in range(ROWS):
        s_diag = dot(ones, jnp.where(eye, s_buf[r], zero))
        m_diag = dot(ones, jnp.where(eye, m_buf[r], zero))
        dynamic = s_diag - factor * m_diag
        at = slice(r * BLK, (r + 1) * BLK)
        inverse = 1.0 / dynamic
        disp = l_buf[:, at] * inverse
        dyn_o[:, at] = dynamic
        inv_o[:, at] = inverse
        inner_o[r] = disp.astype(BF16)
        parts[: 3 * OWN, at] = split3(disp)
        parts[3 * OWN :, at] = split3(dynamic)
    listed = dot(parts[...], hot_o[...])
    mine_o[:OWN, :] = sum3(listed[: 3 * OWN])
    mine_o[INV : INV + OWN, :] = 1.0 / sum3(listed[3 * OWN :])
    put_edges(place, inner_o, even_o, odd_o)
    place_o[0] = place[0]
    place_o[1] = place[1]
    place_o[2] = place[2]
    moves[7].wait()
    moves[8].wait()


def relative_kernel(mine, far, swap, *refs, first, final):
    if first:
        out, swap_far = refs[-2:]
        wanted = far[FACING : FACING + 1, :].astype(jnp.int32)
        swap_far[...] = one_hot(wanted)
        near_disp, far_disp = mine[:OWN, :], far[:OWN, :]
    else:
        swap_far, force, near_lin, far_lin, _, out = refs
        near_disp = near_lin[...] - force[:, :CMAX] * mine[INV : INV + OWN, :]
        far_disp = far_lin[...] - force[:, CMAX:] * far[INV : INV + OWN, :]
    facing = sum3(dot(split3(far_disp), swap[...]))
    out[:, :CMAX] = (near_disp - facing) * mine[RATIO : RATIO + 1, :]
    if not final:
        facing = sum3(dot(split3(near_disp), swap_far[...]))
        out[:, CMAX:] = (far_disp - facing) * far[RATIO : RATIO + 1, :]


def join_kernel(a, b, *rest):
    out = rest[-1]
    n = a.shape[0]
    out[:n, :] = a[...]
    out[n:, :] = b[...]


INSIDE = tuple(range(BAND, ROWS - BAND))
OUTSIDE = tuple(range(BAND)) + tuple(range(ROWS - BAND, ROWS))


def product_kernel(*refs, edges, first, final, more, after):
    refs = list(refs)
    cols, freq, place, inner = refs[:4]
    del refs[:4]
    if edges:
        even, odd = refs[:2]
        del refs[:2]
    if first:
        stiff, mass = refs[:2]
        del refs[:2]
    else:
        wide = refs.pop(0)
    load, hot, scale = refs[:3]
    del refs[:3]
    if final:
        disp = refs.pop(0)
    if more:
        earlier = refs.pop(0)
    del refs[:after]
    lin_o = refs.pop(0)
    if not final:
        listed_o = refs.pop(0)
    if first:
        wide = refs.pop(0)
    field, parts = refs
    own = place[1] * ROWS
    if edges:
        side = lax.rem(place[1], 2)
        far_end = BAND + ROWS
        field[BAND:far_end] = inner[...]
        field[pl.ds((1 - side) * far_end, BAND)] = even[...]
        alone = (place[1] == 0) | (place[1] == place[2] - 1)
        field[pl.ds(side * far_end, BAND)] = jnp.where(alone, jnp.zeros(odd.shape, BF16), odd[...])
        source, offset = field, own - BAND
    else:
        source, offset = inner, own
    factor = own_factor(freq, place)
    chosen = OUTSIDE if edges else INSIDE
    for i, r in enumerate(chosen):
        at = slice(r * BLK, (r + 1) * BLK)
        here = slice(i * BLK, (i + 1) * BLK)
        picked = [source[cols[s, r] - offset] for s in range(SLOTS)]
        if first:
            for s in range(SLOTS):
                wide[i, s * BLK : (s + 1) * BLK, :BLK] = stiff[r, s].T
                wide[i, s * BLK : (s + 1) * BLK, BLK:] = mass[r, s].T
        made = dot(jnp.concatenate(picked, axis=1), wide[i])
        applied = made[:, :BLK] - factor * made[:, BLK:]
        rounded = inner[r].astype(F32)
        if final:
            lin_o[:, here] = load[:, at] - (applied + scale[:, at] * (disp[:, at] - rounded))
        else:
            lin = rounded + (load[:, at] - applied) * scale[:, at]
            lin_o[:, here] = lin
            parts[:, here] = split3(lin)
    if not final:
        if edges:
            cut, tail = BAND * BLK, (ROWS - BAND) * BLK
            made = dot(parts[:, :cut], hot[:cut, :]) + dot(parts[:, cut:], hot[tail:, :])
        else:
            made = dot(parts[...], hot[BAND * BLK : (ROWS - BAND) * BLK, :])
        made = sum3(made)
        listed_o[...] = made + earlier[...] if more else made


def lin_block(inside, outside, r):
    if r in INSIDE:
        i = INSIDE.index(r)
        return inside[:, i * BLK : (i + 1) * BLK]
    i = OUTSIDE.index(r)
    return outside[:, i * BLK : (i + 1) * BLK]


def time_kernel(place, near, opposite, across, forward, backward, mine, far, *rest, final):
    force_o, rel = rest[-2:]
    me, width = place[0], near.shape[1]
    for ref, at, other in (
        (near, 0, 0), (near, 1, 2), (opposite, 0, 6), (opposite, 1, 4),
        (across, 0, 1), (across, 1, 3), (across, 2, 7), (across, 3, 5),
    ):
        to = pl.multiple_of(jnp.bitwise_xor(me, other) * OWN, OWN)
        for c in range(width // BLK):
            rel[c, pl.ds(to, OWN), :] = ref[at * OWN : (at + 1) * OWN, c * BLK : (c + 1) * BLK]
    for first_col in range(0, width, CMAX):
        stacked = []
        for parity in range(2):
            part = jnp.concatenate(
                [rel[first_col // BLK + c, pl.ds(parity, H // 2, stride=2), :] for c in range(CMAX // BLK)], axis=1
            )
            high = part.astype(BF16)
            low = (part - high.astype(F32)).astype(BF16)
            stacked.append(jnp.concatenate([high, low, high], axis=0))
        total = jnp.zeros((2 * OWN, CMAX), F32)
        for n in range(0, TIME_POINTS // 2, BLK):
            even = dot(forward[0, n : n + BLK, :], stacked[0])
            odd = dot(forward[1, n : n + BLK, :], stacked[1])
            values = jnp.concatenate([jnp.tanh(even + odd).astype(BF16), jnp.tanh(even - odd).astype(BF16)], axis=0)
            total = total + dot(backward[:, 2 * n : 2 * n + 2 * BLK], values)
        limit = (far if first_col else mine)[LIMIT : LIMIT + 1, :]
        force_o[:, first_col : first_col + CMAX] = (total[:OWN] + total[OWN:]) * limit


def spread(force, hot_block):
    high = force.astype(BF16)
    low = (force - high.astype(F32)).astype(BF16)
    both = dot_nt(jnp.concatenate([high, low], axis=0), hot_block)
    return both[:OWN] + both[OWN:]


def update_kernel(place, force, hot, lin_a, lin_b, inv, inner_o, even_o, odd_o, *rest):
    add = force[:, :CMAX]
    for r in range(ROWS):
        at = slice(r * BLK, (r + 1) * BLK)
        lin = lin_block(lin_a, lin_b, r)
        disp = lin - spread(add, hot[at, :]) * inv[:, at]
        if rest:
            rest[0][:, at] = disp
        inner_o[r] = disp.astype(BF16)
    put_edges(place, inner_o, even_o, odd_o)


def finish_kernel(force, hot, lin_a, lin_b, inv, disp, disp_o, residual_o, disp_b, residual_b, sems):
    add = force[:, :CMAX]
    moves = []
    for r in range(ROWS):
        at = slice(r * BLK, (r + 1) * BLK)
        residual = lin_block(lin_a, lin_b, r) - spread(add, hot[at, :])
        residual_b[:, at] = residual
        disp_b[:, at] = disp[:, at] + residual * inv[:, at]
        if r % BAND == BAND - 1:
            part, ready = r // BAND, pl.ds((r + 1 - BAND) * BLK, BAND * BLK)
            moves.append(pltpu.make_async_copy(disp_b.at[:, ready], disp_o.at[:, ready], sems.at[0, part]))
            moves.append(pltpu.make_async_copy(residual_b.at[:, ready], residual_o.at[:, ready], sems.at[1, part]))
            for move in moves[-2:]:
                move.start()
    for move in moves:
        move.wait()


def shape(dims, dtype=F32):
    return jax.ShapeDtypeStruct(dims, dtype)


def held(dims, dtype=F32):
    return pltpu.VMEM(dims, dtype)


def params(limit=4):
    return pltpu.CompilerParams(vmem_limit_bytes=limit << 20)


def cost(us):
    return pl.CostEstimate(flops=int(us * 1.0e9), bytes_accessed=int(us * 3.0e6), transcendentals=0)


FULL = (OWN, DOFS)
PART = (OWN, HALF * BLK)
LIST = (OWN, CMAX)
EDGE = (BAND, OWN, BLK)
BLOCKED = (ROWS, OWN, BLK)
WIDE = (HALF, SLOTS * BLK, 2 * BLK)


def local(
    load,
    stiff_blocks,
    mass_blocks,
    block_cols,
    contact_rows,
    partner_slot,
    contact_count,
    normal_load,
    contact_stiffness,
    frequency,
):
    harm = lax.axis_index("harm").astype(jnp.int32)
    comp = lax.axis_index("comp").astype(jnp.int32)
    place = jnp.stack([harm, comp, jnp.int32(lax.axis_size("comp"))])
    groups = lax.axis_size("comp")
    devices = lax.axis_size("harm")
    cols = block_cols.T
    forward, backward = (jnp.asarray(t) for t in tables())
    inner, even, odd, dyn, inv, hot, swap, mine, backward, place, cols = pl.pallas_call(
        init_kernel,
        out_shape=(
            shape(BLOCKED, BF16), shape(EDGE, BF16), shape(EDGE, BF16),
            shape(FULL), shape(FULL), shape((DOFS, CMAX), BF16), shape((CMAX, CMAX), BF16),
            shape((MINE, CMAX)), shape((2 * OWN, TIME_POINTS), BF16),
            pltpu.SMEM((3,), jnp.int32), pltpu.SMEM((SLOTS, ROWS), jnp.int32),
        ),
        in_specs=[SM, SM, SM] + [FAR] * 9,
        out_specs=(VM,) * 9 + (SM,) * 2,
        scratch_shapes=[
            pltpu.VMEM((ROWS, BLK, BLK), BF16),
            pltpu.VMEM((ROWS, BLK, BLK), BF16),
            pltpu.VMEM(FULL, F32),
            pltpu.VMEM((2, 1, CMAX), jnp.int32),
            pltpu.VMEM((2, 1, CMAX), F32),
            pltpu.VMEM((6 * OWN, DOFS), BF16),
            pltpu.SemaphoreType.DMA((9,)),
        ],
        compiler_params=params(),
        cost_estimate=cost(3.0),
        name="init",
    )(
        frequency, place, contact_count, *(
            pltpu.with_memory_space_constraint(x, pltpu.HBM)
            for x in (load, stiff_blocks, mass_blocks, contact_rows, partner_slot, normal_load, contact_stiffness, backward, cols)
        )
    )

    stiff_late, mass_late, _ = lax.optimization_barrier((stiff_blocks, mass_blocks, mine))
    stiff_near = pltpu.with_memory_space_constraint(stiff_late, pltpu.VMEM)
    mass_near = pltpu.with_memory_space_constraint(mass_late, pltpu.VMEM)

    across = groups // 2
    facing = [(i, i ^ across) for i in range(groups)]
    evens = [(i, i ^ 1) for i in range(groups)]
    odds = [(i, (i - 1 + 2 * (i % 2)) % groups) for i in range(groups)]

    def flipped(x, bits):
        return lax.ppermute(x, "harm", [(i, i ^ bits) for i in range(devices)])

    far = lax.ppermute(mine, "comp", facing)
    def join(a, b, *after):
        return pl.pallas_call(
            join_kernel,
            out_shape=shape((2 * a.shape[0], a.shape[1])),
            in_specs=[VM] * (2 + len(after)),
            out_specs=VM,
            compiler_params=params(),
            cost_estimate=cost(0.1),
            name="join",
        )(a, b, *after)

    wides = {}
    for sweep in range(ITERS):
        first, final = sweep == 0, sweep == ITERS - 1
        even_in = lax.ppermute(even, "comp", evens)
        odd_in = lax.ppermute(odd, "comp", odds)

        def product(edges, extra, after=()):
            take = [cols, frequency, place, inner] + ([even_in, odd_in] if edges else [])
            if first:
                take += [stiff_near, mass_near]
            else:
                take += [pltpu.with_memory_space_constraint(wides[edges], pltpu.VMEM)]
            take += [load, hot, dyn if final else inv]
            take += ([kept] if final else []) + [*extra, *after]
            give = [shape(PART)] + ([] if final else [shape(LIST)]) + ([held(WIDE, BF16)] if first else [])
            outs = pl.pallas_call(
                functools.partial(
                    product_kernel, edges=edges, first=first, final=final, more=bool(extra), after=len(after)
                ),
                out_shape=tuple(give),
                in_specs=[SM] * 3 + [VM] * (len(take) - 3),
                out_specs=(VM,) * len(give),
                scratch_shapes=[
                    pltpu.VMEM((ROWS + 2 * BAND, OWN, BLK), BF16),
                    pltpu.VMEM((3 * OWN, HALF * BLK), BF16),
                ],
                compiler_params=params(),
                cost_estimate=cost(3.0 if first else 1.5),
                name="edges" if edges else "inside",
            )(*take)
            if first:
                wides[edges] = outs[-1]
            return outs[:1] if final else outs[:2]

        wide_list = LIST if final else (OWN, 2 * CMAX)
        given = [mine, far, swap] + ([even_in] if first else [swap_far, force, near_lin, far_lin, inner])
        made = pl.pallas_call(
            functools.partial(relative_kernel, first=first, final=final),
            out_shape=(shape(wide_list),) + ((shape((CMAX, CMAX), BF16),) if first else ()),
            in_specs=[VM] * len(given),
            out_specs=(VM,) * (2 if first else 1),
            compiler_params=params(),
            cost_estimate=cost(0.2),
            name="relative",
        )(*given)
        relative = made[0]
        if first:
            swap_far = made[1]
        beside = flipped(relative, 2)
        if first:
            inside = product(False, [])
            near = join(relative, beside, inside[0])
            outside = product(True, inside[1:], [near])
        else:
            near = join(relative, beside)
            inside = product(False, [], [near])
            outside = product(True, inside[1:])
        added = outside
        opposite = flipped(near, 6)
        across_core = flipped(join(near, opposite, inside[0], *([] if final else outside[:1])), 1)
        lins = [inside[0], outside[0]]
        if not final:
            near_lin = added[1]
            far_lin = lax.ppermute(near_lin, "comp", facing)
        given = [near, opposite, across_core, forward, backward, mine, far]
        force = pl.pallas_call(
            functools.partial(time_kernel, final=final),
            out_shape=shape(wide_list),
            in_specs=[SM] + [VM] * len(given),
            out_specs=VM,
            scratch_shapes=[pltpu.VMEM((wide_list[1] // BLK, H, BLK), F32)],
            compiler_params=params(),
            cost_estimate=cost(0.01),
            name="time",
        )(place, *given)
        if final:
            return pl.pallas_call(
                finish_kernel,
                out_shape=(shape(FULL), shape(FULL)),
                in_specs=[VM] * 6,
                out_specs=(FAR, FAR),
                scratch_shapes=[
                    pltpu.VMEM(FULL, F32),
                    pltpu.VMEM(FULL, F32),
                    pltpu.SemaphoreType.DMA((2, ROWS // BAND)),
                ],
                compiler_params=params(),
                name="finish",
            )(force, hot, *lins, inv, kept)
        keep = (shape(FULL),) if sweep == ITERS - 2 else ()
        inner, even, odd, *rest = pl.pallas_call(
            update_kernel,
            out_shape=(shape(BLOCKED, BF16), shape(EDGE, BF16), shape(EDGE, BF16)) + keep,
            in_specs=[SM] + [VM] * 5,
            out_specs=(VM,) * (3 + len(keep)),
            compiler_params=params(),
            cost_estimate=cost(0.01),
            name="update",
        )(place, force, hot, *lins, inv)
        if rest:
            kept = rest[0]


def solution(mesh):
    placed = (
        P("harm", "comp"),
        P("comp", None, None, None),
        P("comp", None, None, None),
        P("comp", None),
        P("comp", None),
        P("comp", None),
        P("comp"),
        P("comp", None),
        P("comp", None),
        P(),
    )
    return jax.shard_map(
        local,
        mesh=mesh,
        in_specs=placed,
        out_specs=(P("harm", "comp"), P("harm", "comp")),
        check_vma=False,
    )
```

```python
import functools
import math

import jax
import jax.numpy as jnp
import ml_dtypes
import numpy as np
from jax import lax
from jax.experimental import pallas as pl
from jax.experimental.pallas import tpu as pltpu
from jax.sharding import PartitionSpec as P

H = 128
TIME_POINTS = 1024
BLK = 128
SLOTS = 8
BAND = 8
ITERS = 3
OWN = 16
ROWS = 32
HALF = ROWS // 2
RATIO = 16
LIMIT = 17
FACING = 18
STIFF = 19
MASS = 20
MINE = 32
STEP = 8
CMAX = 256
DOFS = ROWS * BLK
F32 = jnp.float32
BF16 = jnp.bfloat16
LAST_LAST = (((1,), (1,)), ((), ()))

VM = pl.BlockSpec(memory_space=pltpu.VMEM)
SM = pl.BlockSpec(memory_space=pltpu.SMEM)
FAR = pl.BlockSpec(memory_space=pltpu.HBM)


def tables():
    j = np.arange(H)
    waves = np.where(j <= H // 2, j, j - H // 2)
    phase = (np.arange(TIME_POINTS)[:, None] * waves[None, :]) % TIME_POINTS
    angle = phase.astype(np.float64) * (2.0 * math.pi / TIME_POINTS)
    table = np.where(j[None, :] <= H // 2, np.cos(angle), np.sin(angle)).astype(np.float32)
    high = table.astype(ml_dtypes.bfloat16)
    low = (table - high.astype(np.float32)).astype(ml_dtypes.bfloat16)
    half = TIME_POINTS // 2
    forward = np.stack(
        [
            np.concatenate([high[:half, p::2], high[:half, p::2], low[:half, p::2]], axis=1)
            for p in range(2)
        ]
    )
    weights = (np.where(j == 0, 1.0, 2.0) / TIME_POINTS).astype(np.float32)
    back = (table * weights[None, :]).T
    back_high = back.astype(ml_dtypes.bfloat16)
    back_low = (back - back_high.astype(np.float32)).astype(ml_dtypes.bfloat16)
    order = np.arange(TIME_POINTS).reshape(2, -1, BLK).transpose(1, 0, 2).reshape(-1)
    back_high, back_low = back_high[:, order], back_low[:, order]
    backward = np.concatenate(
        [
            back_high.reshape(H // OWN, OWN, TIME_POINTS),
            back_low.reshape(H // OWN, OWN, TIME_POINTS),
        ],
        axis=1,
    )
    return forward, backward


def dot(a, b):
    return jnp.dot(a, b, preferred_element_type=F32)


def dot_nt(a, b):
    return lax.dot_general(a, b, LAST_LAST, preferred_element_type=F32)


def split3(x):
    high = x.astype(BF16)
    rest = x - high.astype(F32)
    mid = rest.astype(BF16)
    low = (rest - mid.astype(F32)).astype(BF16)
    return jnp.concatenate([high, mid, low], axis=0)


def sum3(y):
    n = y.shape[0] // 3
    return y[:n] + y[n : 2 * n] + y[2 * n :]


def own_factor(freq, place):
    j = place[0] * OWN + lax.broadcasted_iota(jnp.int32, (OWN, BLK), 0)
    waves = jnp.where(j <= H // 2, j, j - H // 2)
    factor = freq[0] * waves.astype(F32) * (2.0 / H)
    return factor * factor


def cols_of(r):
    return pl.ds(pl.multiple_of(r * BLK, BLK), BLK)


def put_edges(place, inner, even_o, odd_o):
    low, high = slice(0, BAND), slice(ROWS - BAND, ROWS)
    side = lax.rem(place[1], 2)

    @pl.when(side == 0)
    def _():
        even_o[...] = inner[high]
        odd_o[...] = inner[low]

    @pl.when(side == 1)
    def _():
        even_o[...] = inner[low]
        odd_o[...] = inner[high]


def one_hot(wanted):
    row = lax.broadcasted_iota(jnp.int32, (CMAX, CMAX), 0)
    return jnp.where(row == wanted, 1.0, 0.0).astype(BF16)


def init_kernel(
    freq, place, count, load, stiff, mass, rows, pslot, normal, tangent, backward, cols,
    inner_o, even_o, odd_o, dyn_o, inv_o, hot_o, swap_o, mine_o, backward_o, place_o, cols_o,
    s_buf, m_buf, l_buf, small_i, small_f, parts, sems,
):
    moves = [
        pltpu.make_async_copy(rows, small_i.at[0], sems.at[0]),
        pltpu.make_async_copy(pslot, small_i.at[1], sems.at[1]),
        pltpu.make_async_copy(normal, small_f.at[0], sems.at[2]),
        pltpu.make_async_copy(tangent, small_f.at[1], sems.at[3]),
        pltpu.make_async_copy(stiff.at[:, 0], s_buf, sems.at[4]),
        pltpu.make_async_copy(mass.at[:, 0], m_buf, sems.at[5]),
        pltpu.make_async_copy(load, l_buf, sems.at[6]),
        pltpu.make_async_copy(backward.at[place[0]], backward_o, sems.at[7]),
        pltpu.make_async_copy(cols, cols_o, sems.at[8]),
    ]
    for move in moves:
        move.start()
    factor = own_factor(freq, place)
    for move in moves[:4]:
        move.wait()
    in_block = lax.broadcasted_iota(jnp.int32, (BLK, CMAX), 0)
    wanted = small_i[0]
    for r in range(ROWS):
        hot_o[r * BLK : (r + 1) * BLK, :] = jnp.where(in_block + r * BLK == wanted, 1.0, 0.0).astype(BF16)
    swap_o[...] = one_hot(small_i[1])
    live = lax.broadcasted_iota(jnp.int32, (1, CMAX), 1) < count[0]
    mine_o[OWN:, :] = jnp.zeros((MINE - OWN, CMAX), F32)
    mine_o[RATIO : RATIO + 1, :] = small_f[1] / small_f[0]
    mine_o[LIMIT : LIMIT + 1, :] = jnp.where(live, small_f[0], 0.0)
    mine_o[FACING : FACING + 1, :] = small_i[1].astype(F32)
    eye = lax.broadcasted_iota(jnp.int32, (BLK, BLK), 0) == lax.broadcasted_iota(
        jnp.int32, (BLK, BLK), 1
    )
    ones = jnp.ones((OWN, BLK), BF16)
    upper = lax.broadcasted_iota(jnp.int32, (OWN, BLK), 0) < OWN // 2
    zero = jnp.zeros((BLK, BLK), BF16)
    for move in moves[4:7]:
        move.wait()
    for r in range(ROWS):
        s_diag = dot(ones, jnp.where(eye, s_buf[r], zero))
        m_diag = dot(ones, jnp.where(eye, m_buf[r], zero))
        dynamic = s_diag - factor * m_diag
        at = slice(r * BLK, (r + 1) * BLK)
        inverse = 1.0 / dynamic
        disp = l_buf[:, at] * inverse
        dyn_o[:, at] = dynamic
        inv_o[:, at] = inverse
        inner_o[r] = disp.astype(BF16)
        parts[: 3 * OWN, at] = split3(disp)
        parts[3 * OWN :, at] = jnp.where(upper, s_diag, m_diag).astype(BF16)
    listed = dot(parts[...], hot_o[...])
    mine_o[:OWN, :] = sum3(listed[: 3 * OWN])
    mine_o[STIFF : STIFF + 1, :] = listed[3 * OWN : 3 * OWN + 1]
    mine_o[MASS : MASS + 1, :] = listed[4 * OWN - 1 :]
    put_edges(place, inner_o, even_o, odd_o)
    place_o[0] = place[0]
    place_o[1] = place[1]
    place_o[2] = place[2]
    moves[7].wait()
    moves[8].wait()


def relative_kernel(freq, place, mine, far, swap, *refs, first, final):
    if first:
        out, swap_far = refs[-2:]
        wanted = far[FACING : FACING + 1, :].astype(jnp.int32)
        swap_far[...] = one_hot(wanted)
        near_disp, far_disp = mine[:OWN, :], far[:OWN, :]
    else:
        swap_far, force, near_lin, far_lin, _, out = refs
        factor = own_factor(freq, place)
        factor = jnp.concatenate([factor, factor], axis=1)
        near_dyn = mine[STIFF : STIFF + 1, :] - factor * mine[MASS : MASS + 1, :]
        far_dyn = far[STIFF : STIFF + 1, :] - factor * far[MASS : MASS + 1, :]
        near_disp = near_lin[...] - force[:, :CMAX] / near_dyn
        far_disp = far_lin[...] - force[:, CMAX:] / far_dyn
    facing = sum3(dot(split3(far_disp), swap[...]))
    out[:, :CMAX] = (near_disp - facing) * mine[RATIO : RATIO + 1, :]
    if not final:
        facing = sum3(dot(split3(near_disp), swap_far[...]))
        out[:, CMAX:] = (far_disp - facing) * far[RATIO : RATIO + 1, :]


def join_kernel(a, b, *rest):
    out = rest[-1]
    n = a.shape[0]
    out[:n, :] = a[...]
    out[n:, :] = b[...]


INSIDE = tuple(range(BAND, ROWS - BAND))
OUTSIDE = tuple(range(BAND)) + tuple(range(ROWS - BAND, ROWS))


def product_kernel(*refs, edges, first, final, more, after):
    refs = list(refs)
    cols, freq, place, inner = refs[:4]
    del refs[:4]
    if edges:
        even, odd = refs[:2]
        del refs[:2]
    if first:
        stiff, mass = refs[:2]
        del refs[:2]
    else:
        wide = refs.pop(0)
    load, hot, scale = refs[:3]
    del refs[:3]
    if final:
        disp = refs.pop(0)
    if more:
        earlier = refs.pop(0)
    del refs[:after]
    lin_o = refs.pop(0)
    if not final:
        listed_o = refs.pop(0)
    if first:
        wide = refs.pop(0)
    field, parts = refs
    own = place[1] * ROWS
    if edges:
        side = lax.rem(place[1], 2)
        far_end = BAND + ROWS
        field[BAND:far_end] = inner[...]
        field[pl.ds((1 - side) * far_end, BAND)] = even[...]
        alone = (place[1] == 0) | (place[1] == place[2] - 1)
        field[pl.ds(side * far_end, BAND)] = jnp.where(alone, jnp.zeros(odd.shape, BF16), odd[...])
        source, offset = field, own - BAND
    else:
        source, offset = inner, own
    factor = own_factor(freq, place)
    chosen = OUTSIDE if edges else INSIDE
    for i, r in enumerate(chosen):
        at = slice(r * BLK, (r + 1) * BLK)
        here = slice(i * BLK, (i + 1) * BLK)
        picked = [source[cols[s, r] - offset] for s in range(SLOTS)]
        if first:
            for s in range(SLOTS):
                wide[i, s * BLK : (s + 1) * BLK, :BLK] = stiff[r, s].T
                wide[i, s * BLK : (s + 1) * BLK, BLK:] = mass[r, s].T
        made = dot(jnp.concatenate(picked, axis=1), wide[i])
        applied = made[:, :BLK] - factor * made[:, BLK:]
        rounded = inner[r].astype(F32)
        if final:
            lin_o[:, here] = load[:, at] - (applied + scale[:, at] * (disp[:, at] - rounded))
        else:
            lin = rounded + (load[:, at] - applied) * scale[:, at]
            lin_o[:, here] = lin
            parts[:, here] = split3(lin)
    if not final:
        if edges:
            cut, tail = BAND * BLK, (ROWS - BAND) * BLK
            made = dot(parts[:, :cut], hot[:cut, :]) + dot(parts[:, cut:], hot[tail:, :])
        else:
            made = dot(parts[...], hot[BAND * BLK : (ROWS - BAND) * BLK, :])
        made = sum3(made)
        listed_o[...] = made + earlier[...] if more else made


def lin_block(inside, outside, r):
    if r in INSIDE:
        i = INSIDE.index(r)
        return inside[:, i * BLK : (i + 1) * BLK]
    i = OUTSIDE.index(r)
    return outside[:, i * BLK : (i + 1) * BLK]


def time_kernel(place, near, opposite, across, forward, backward, mine, far, *rest, final):
    force_o, rel = rest[-2:]
    me, width = place[0], near.shape[1]
    for ref, at, other in (
        (near, 0, 0), (near, 1, 2), (opposite, 0, 6), (opposite, 1, 4),
        (across, 0, 1), (across, 1, 3), (across, 2, 7), (across, 3, 5),
    ):
        to = pl.multiple_of(jnp.bitwise_xor(me, other) * OWN, OWN)
        for c in range(width // BLK):
            rel[c, pl.ds(to, OWN), :] = ref[at * OWN : (at + 1) * OWN, c * BLK : (c + 1) * BLK]
    for first_col in range(0, width, CMAX):
        stacked = []
        for parity in range(2):
            part = jnp.concatenate(
                [rel[first_col // BLK + c, pl.ds(parity, H // 2, stride=2), :] for c in range(CMAX // BLK)], axis=1
            )
            high = part.astype(BF16)
            low = (part - high.astype(F32)).astype(BF16)
            stacked.append(jnp.concatenate([high, low, high], axis=0))
        total = jnp.zeros((2 * OWN, CMAX), F32)
        for n in range(0, TIME_POINTS // 2, BLK):
            even = dot(forward[0, n : n + BLK, :], stacked[0])
            odd = dot(forward[1, n : n + BLK, :], stacked[1])
            values = jnp.concatenate([jnp.tanh(even + odd).astype(BF16), jnp.tanh(even - odd).astype(BF16)], axis=0)
            total = total + dot(backward[:, 2 * n : 2 * n + 2 * BLK], values)
        limit = (far if first_col else mine)[LIMIT : LIMIT + 1, :]
        force_o[:, first_col : first_col + CMAX] = (total[:OWN] + total[OWN:]) * limit


def spread(force, hot_block):
    high = force.astype(BF16)
    low = (force - high.astype(F32)).astype(BF16)
    both = dot_nt(jnp.concatenate([high, low], axis=0), hot_block)
    return both[:OWN] + both[OWN:]


def update_kernel(place, force, hot, lin_a, lin_b, inv, inner_o, even_o, odd_o, *rest):
    add = force[:, :CMAX]
    for r in range(ROWS):
        at = slice(r * BLK, (r + 1) * BLK)
        lin = lin_block(lin_a, lin_b, r)
        disp = lin - spread(add, hot[at, :]) * inv[:, at]
        if rest:
            rest[0][:, at] = disp
        inner_o[r] = disp.astype(BF16)
    put_edges(place, inner_o, even_o, odd_o)


def finish_kernel(force, hot, lin_a, lin_b, inv, disp, disp_o, residual_o, disp_b, residual_b, sems):
    add = force[:, :CMAX]
    moves = []
    for r in range(ROWS):
        at = slice(r * BLK, (r + 1) * BLK)
        residual = lin_block(lin_a, lin_b, r) - spread(add, hot[at, :])
        residual_b[:, at] = residual
        disp_b[:, at] = disp[:, at] + residual * inv[:, at]
        if r % STEP == STEP - 1:
            part, ready = r // STEP, pl.ds((r + 1 - STEP) * BLK, STEP * BLK)
            moves.append(pltpu.make_async_copy(disp_b.at[:, ready], disp_o.at[:, ready], sems.at[0, part]))
            moves.append(pltpu.make_async_copy(residual_b.at[:, ready], residual_o.at[:, ready], sems.at[1, part]))
            for move in moves[-2:]:
                move.start()
    for move in moves:
        move.wait()


def shape(dims, dtype=F32):
    return jax.ShapeDtypeStruct(dims, dtype)


def held(dims, dtype=F32):
    return pltpu.VMEM(dims, dtype)


def params(limit=4):
    return pltpu.CompilerParams(vmem_limit_bytes=limit << 20)


def cost(us):
    return pl.CostEstimate(flops=int(us * 1.0e9), bytes_accessed=int(us * 3.0e6), transcendentals=0)


FULL = (OWN, DOFS)
PART = (OWN, HALF * BLK)
LIST = (OWN, CMAX)
EDGE = (BAND, OWN, BLK)
BLOCKED = (ROWS, OWN, BLK)
WIDE = (HALF, SLOTS * BLK, 2 * BLK)


def local(
    load,
    stiff_blocks,
    mass_blocks,
    block_cols,
    contact_rows,
    partner_slot,
    contact_count,
    normal_load,
    contact_stiffness,
    frequency,
):
    harm = lax.axis_index("harm").astype(jnp.int32)
    comp = lax.axis_index("comp").astype(jnp.int32)
    place = jnp.stack([harm, comp, jnp.int32(lax.axis_size("comp"))])
    groups = lax.axis_size("comp")
    devices = lax.axis_size("harm")
    cols = block_cols.T
    forward, backward = (jnp.asarray(t) for t in tables())
    inner, even, odd, dyn, inv, hot, swap, mine, backward, place, cols = pl.pallas_call(
        init_kernel,
        out_shape=(
            shape(BLOCKED, BF16), shape(EDGE, BF16), shape(EDGE, BF16),
            shape(FULL), shape(FULL), shape((DOFS, CMAX), BF16), shape((CMAX, CMAX), BF16),
            shape((MINE, CMAX)), shape((2 * OWN, TIME_POINTS), BF16),
            pltpu.SMEM((3,), jnp.int32), pltpu.SMEM((SLOTS, ROWS), jnp.int32),
        ),
        in_specs=[SM, SM, SM] + [FAR] * 9,
        out_specs=(VM,) * 9 + (SM,) * 2,
        scratch_shapes=[
            pltpu.VMEM((ROWS, BLK, BLK), BF16),
            pltpu.VMEM((ROWS, BLK, BLK), BF16),
            pltpu.VMEM(FULL, F32),
            pltpu.VMEM((2, 1, CMAX), jnp.int32),
            pltpu.VMEM((2, 1, CMAX), F32),
            pltpu.VMEM((4 * OWN, DOFS), BF16),
            pltpu.SemaphoreType.DMA((9,)),
        ],
        compiler_params=params(),
        cost_estimate=cost(3.0),
        name="init",
    )(
        frequency, place, contact_count, *(
            pltpu.with_memory_space_constraint(x, pltpu.HBM)
            for x in (load, stiff_blocks, mass_blocks, contact_rows, partner_slot, normal_load, contact_stiffness, backward, cols)
        )
    )

    stiff_late, mass_late, _ = lax.optimization_barrier((stiff_blocks, mass_blocks, mine))
    stiff_near = pltpu.with_memory_space_constraint(stiff_late, pltpu.VMEM)
    mass_near = pltpu.with_memory_space_constraint(mass_late, pltpu.VMEM)

    across = groups // 2
    facing = [(i, i ^ across) for i in range(groups)]
    evens = [(i, i ^ 1) for i in range(groups)]
    odds = [(i, (i - 1 + 2 * (i % 2)) % groups) for i in range(groups)]

    def flipped(x, bits):
        return lax.ppermute(x, "harm", [(i, i ^ bits) for i in range(devices)])

    far = lax.ppermute(mine, "comp", facing)
    def join(a, b, *after):
        return pl.pallas_call(
            join_kernel,
            out_shape=shape((2 * a.shape[0], a.shape[1])),
            in_specs=[VM] * (2 + len(after)),
            out_specs=VM,
            compiler_params=params(),
            cost_estimate=cost(0.1),
            name="join",
        )(a, b, *after)

    wides = {}
    for sweep in range(ITERS):
        first, final = sweep == 0, sweep == ITERS - 1
        even_in = lax.ppermute(even, "comp", evens)
        odd_in = lax.ppermute(odd, "comp", odds)

        def product(edges, extra, after=()):
            take = [cols, frequency, place, inner] + ([even_in, odd_in] if edges else [])
            if first:
                take += [stiff_near, mass_near]
            else:
                take += [pltpu.with_memory_space_constraint(wides[edges], pltpu.VMEM)]
            take += [load, hot, dyn if final else inv]
            take += ([kept] if final else []) + [*extra, *after]
            give = [shape(PART)] + ([] if final else [shape(LIST)]) + ([held(WIDE, BF16)] if first else [])
            outs = pl.pallas_call(
                functools.partial(
                    product_kernel, edges=edges, first=first, final=final, more=bool(extra), after=len(after)
                ),
                out_shape=tuple(give),
                in_specs=[SM] * 3 + [VM] * (len(take) - 3),
                out_specs=(VM,) * len(give),
                scratch_shapes=[
                    pltpu.VMEM((ROWS + 2 * BAND, OWN, BLK), BF16),
                    pltpu.VMEM((3 * OWN, HALF * BLK), BF16),
                ],
                compiler_params=params(),
                cost_estimate=cost(3.0 if first else 1.5),
                name="edges" if edges else "inside",
            )(*take)
            if first:
                wides[edges] = outs[-1]
            return outs[:1] if final else outs[:2]

        wide_list = LIST if final else (OWN, 2 * CMAX)
        given = [mine, far, swap] + ([even_in] if first else [swap_far, force, near_lin, far_lin, inner])
        made = pl.pallas_call(
            functools.partial(relative_kernel, first=first, final=final),
            out_shape=(shape(wide_list),) + ((shape((CMAX, CMAX), BF16),) if first else ()),
            in_specs=[SM, SM] + [VM] * len(given),
            out_specs=(VM,) * (2 if first else 1),
            compiler_params=params(),
            cost_estimate=cost(0.2),
            name="relative",
        )(frequency, place, *given)
        relative = made[0]
        if first:
            swap_far = made[1]
        beside = flipped(relative, 2)
        if first:
            inside = product(False, [])
            near = join(relative, beside, inside[0])
            outside = product(True, inside[1:], [near])
        else:
            near = join(relative, beside)
            inside = product(False, [], [near])
            outside = product(True, inside[1:])
        added = outside
        opposite = flipped(near, 6)
        across_core = flipped(join(near, opposite, inside[0], *([] if final else outside[:1])), 1)
        lins = [inside[0], outside[0]]
        if not final:
            near_lin = added[1]
            far_lin = lax.ppermute(near_lin, "comp", facing)
        given = [near, opposite, across_core, forward, backward, mine, far]
        force = pl.pallas_call(
            functools.partial(time_kernel, final=final),
            out_shape=shape(wide_list),
            in_specs=[SM] + [VM] * len(given),
            out_specs=VM,
            scratch_shapes=[pltpu.VMEM((wide_list[1] // BLK, H, BLK), F32)],
            compiler_params=params(),
            cost_estimate=cost(0.01),
            name="time",
        )(place, *given)
        if final:
            return pl.pallas_call(
                finish_kernel,
                out_shape=(shape(FULL), shape(FULL)),
                in_specs=[VM] * 6,
                out_specs=(FAR, FAR),
                scratch_shapes=[
                    pltpu.VMEM(FULL, F32),
                    pltpu.VMEM(FULL, F32),
                    pltpu.SemaphoreType.DMA((2, ROWS // STEP)),
                ],
                compiler_params=params(),
                name="finish",
            )(force, hot, *lins, inv, kept)
        keep = (shape(FULL),) if sweep == ITERS - 2 else ()
        inner, even, odd, *rest = pl.pallas_call(
            update_kernel,
            out_shape=(shape(BLOCKED, BF16), shape(EDGE, BF16), shape(EDGE, BF16)) + keep,
            in_specs=[SM] + [VM] * 5,
            out_specs=(VM,) * (3 + len(keep)),
            compiler_params=params(),
            cost_estimate=cost(0.01),
            name="update",
        )(place, force, hot, *lins, inv)
        if rest:
            kept = rest[0]


def solution(mesh):
    placed = (
        P("harm", "comp"),
        P("comp", None, None, None),
        P("comp", None, None, None),
        P("comp", None),
        P("comp", None),
        P("comp", None),
        P("comp"),
        P("comp", None),
        P("comp", None),
        P(),
    )
    return jax.shard_map(
        local,
        mesh=mesh,
        in_specs=placed,
        out_specs=(P("harm", "comp"), P("harm", "comp")),
        check_vma=False,
    )
```
